32 devices in a mesh: row: 4 (over y, x), col: 4 (over z), chan: 2 (over core).
Axes of the slice: x: 2, y: 2, z: 4, core: 2. Of those that a mesh axis runs over, the one named last changes fastest.
Arguments:
- samples: bfloat16 [8192, 2, 2048], P(('chan', 'col'), None, 'row'), parts along dimension 0, may hold values from -6 to 6
- sky_model: bfloat16 [8192, 2, 4096], P(('chan', 'row'), None, 'col'), parts along dimension 0, may hold values from -128 to 128, as said below
- initial_gains: float32 [2, 8192], P(None, ('chan', 'row', 'col')), parts along dimension 1, may hold values from -3 to 3, as said below
Outputs:
- calibrated: float32 [2, 8192], P(None, ('chan', 'row', 'col')), parts along dimension 1
The draws below stay inside these ranges and needn't reach their ends.
There are 2 independent parts, one for each index of `chan`. The reference program is written for one: setup_inputs(seed, part) draws one part's arguments, and reference() takes and returns one part's arrays. A program takes and returns all parts, laid end to end along the dimension named above; each array names one. Nothing has to cross between parts.
Inputs may be any that keep to these rules, and one draw needn't show every extreme that they name: sky_model is Hermitian: sky_model[q,0,p] = sky_model[p,0,q] and sky_model[q,1,p] = -sky_model[p,1,q]. `initial_gains`: every initial gain has magnitude between 0.3 and 3.
All inputs are finite; a program needn't handle non-finite values.
Results may differ from the reference program's by a relative error of at most 0.0003.
Values may be sent and summed in bfloat16 or wider, within the bound.
A program may use at most 192 MiB of HBM per device.

```python
import math
import jax
import jax.numpy as jnp
from jax import lax

ANTENNA_NUMBER = 4096
ITERS = 3
TIME_SAMPLES = 2048


def antenna_scales(key):
    lower_limit = 0.5
    upper_limit = 2.0
    linear_ramp = 1.0 + 2.0 * jnp.arange(ANTENNA_NUMBER, dtype=jnp.float32) / max(ANTENNA_NUMBER - 1, 1)
    gain_spread = jnp.exp(jax.random.uniform(key, (ANTENNA_NUMBER,), jnp.float32, math.log(lower_limit), math.log(upper_limit)))
    return linear_ramp * gain_spread


def draw_sky_model(key, part):
    primary_key, secondary_key = jax.random.split(jax.random.fold_in(key, 11))
    scales = antenna_scales(primary_key)
    baseline_level = jax.random.truncated_normal(secondary_key, -3.0, 3.0, (2, ANTENNA_NUMBER, ANTENNA_NUMBER), jnp.float32)
    real_part = (baseline_level[0] + baseline_level[0].T) * 0.5
    imag_part = (baseline_level[1] - baseline_level[1].T) * 0.5
    outer = scales[:, None] * scales[None, :]
    return jnp.stack([real_part * outer, imag_part * outer], axis=1).astype(jnp.bfloat16)


def draw_initial_gains(key, part):
    primary_key, secondary_key = jax.random.split(jax.random.fold_in(key, 23))
    lower_limit = 0.5
    upper_limit = 2.0
    gain_amplitude = jnp.exp(jax.random.uniform(primary_key, (ANTENNA_NUMBER,), jnp.float32, math.log(lower_limit), math.log(upper_limit)))
    gain_phase = jax.random.uniform(secondary_key, (ANTENNA_NUMBER,), jnp.float32, -math.pi, math.pi)
    return jnp.stack([gain_amplitude * jnp.cos(gain_phase), gain_amplitude * jnp.sin(gain_phase)]).astype(jnp.float32)


def shard_levels(stream_key, dims, cuts, least, largest):
    loudness = 1.0
    for position, blocks in cuts:
        heights = jax.random.uniform(jax.random.fold_in(jax.random.fold_in(stream_key, 6), position), (blocks,), jnp.float32, least / len(cuts), largest / len(cuts))
        loudness = loudness * jnp.repeat(jnp.exp(heights), dims[position] // blocks).reshape((-1,) + (1,) * (len(dims) - 1 - position))
    return loudness


def gaussian(key, shape, deviation, most, pieces=(), kind=jnp.bfloat16):
    array = jax.random.normal(key, shape, jnp.float32) * deviation
    if len(pieces) > 0:
        array = shard_levels(key, shape, pieces, -0.22, 0.18) * array
    return jnp.clip(array, min=-most, max=most).astype(kind)


def setup_inputs(seed: int = 0, part: int = 0) -> dict:
    streams_of = jax.random.split(jax.random.key(seed), 4)
    part_keys = jax.random.split(jax.random.fold_in(streams_of[3], part), 4)
    return {
        "samples": gaussian(part_keys[0], (ANTENNA_NUMBER, 2, TIME_SAMPLES), 1.0, 6.0, ((0, 4), (2, 4))),
        "sky_model": draw_sky_model(jax.random.fold_in(jax.random.fold_in(streams_of[3], part), 71), part),
        "initial_gains": draw_initial_gains(jax.random.fold_in(jax.random.fold_in(streams_of[3], part), 71), part),
    }


def reference(samples, sky_model, initial_gains):
    antennas = samples.shape[0]
    flattened = samples.reshape(antennas, -1)
    rotated = jnp.concatenate([-samples[:, 1, :], samples[:, 0, :]], axis=1)
    vis_real = jnp.dot(flattened, flattened.T, preferred_element_type=jnp.float32)
    vis_imag = jnp.dot(flattened, rotated.T, preferred_element_type=jnp.float32)
    model_real = sky_model[:, 0, :].astype(jnp.float32)
    model_imag = sky_model[:, 1, :].astype(jnp.float32)
    cross_mask = 1.0 - jnp.eye(antennas, dtype=jnp.float32)
    weight_real = (vis_real * model_real + vis_imag * model_imag) * cross_mask
    weight_imag = (vis_real * model_imag - vis_imag * model_real) * cross_mask
    model_power = (model_real * model_real + model_imag * model_imag) * cross_mask
    upper_limit = lax.Precision.HIGHEST
    gain_real = initial_gains[0]
    gain_imag = initial_gains[1]
    for iteration in range(ITERS):
        numer_real = jnp.dot(gain_real, weight_real, precision=upper_limit) - jnp.dot(gain_imag, weight_imag, precision=upper_limit)
        numer_imag = jnp.dot(gain_imag, weight_real, precision=upper_limit) + jnp.dot(gain_real, weight_imag, precision=upper_limit)
        energy = jnp.dot(gain_real * gain_real + gain_imag * gain_imag, model_power, precision=upper_limit)
        new_real = numer_real / energy
        new_imag = numer_imag / energy
        if iteration == 1:
            new_real = 0.5 * (new_real + gain_real)
            new_imag = 0.5 * (new_imag + gain_imag)
        gain_real = new_real
        gain_imag = new_imag
    return jnp.stack([gain_real, gain_imag])
```

```python
import functools

import jax
import jax.numpy as jnp
from jax import lax
from jax.experimental import pallas as pl
from jax.experimental.pallas import tpu as pltpu
from jax.sharding import PartitionSpec as P

ITERS = 3
MESH = pl.DeviceIdType.MESH
CONTRACT_LAST = (((1,), (1,)), ((), ()))


def remote(src, dst, send, recv, row, col):
    return pltpu.make_async_remote_copy(
        src_ref=src,
        dst_ref=dst,
        send_sem=send,
        recv_sem=recv,
        device_id={"row": row, "col": col},
        device_id_type=MESH,
    )


def landed(ref, sem):
    pltpu.make_async_copy(ref, ref, sem).wait()


def calibrate(
    n, own, model, gains, out, chain, left, right, vr, vi, power, qr, qi, tr, ti, gp0, gq0,
    abuf, bbuf, ain, bin_, gin,
    up_send, fwd_send, chain_recv, left_send, left_recv, right_send, right_recv, local_sem,
    gp_send, gp_recv, gq_send, gq_recv, a_send, a_recv, b_send, b_recv, g_send, g_recv,
):
    r = lax.axis_index("row")
    c = lax.axis_index("col")
    block = own.shape[1]
    half = own.shape[2] // 2
    share = gains.shape[1]
    diag = r == c
    off = r != c

    barrier = pltpu.get_barrier_semaphore()
    for step in range(1, n * n):
        other = lax.rem(r * n + c + step, n * n)
        pl.semaphore_signal(
            barrier, inc=1, device_id={"row": other // n, "col": lax.rem(other, n)}, device_id_type=MESH
        )
    pl.semaphore_wait(barrier, n * n - 1)

    up = remote(own.at[0], chain.at[c], up_send.at[0], chain_recv.at[c], r, c + 1)
    down = remote(own.at[1], chain.at[c], up_send.at[1], chain_recv.at[c], r, c - 1)
    pl.when(c < n - 1)(up.start)
    pl.when(c > 0)(down.start)

    def right_copy(k):
        h = jnp.where(k < c, 0, 1)
        return remote(own.at[h], right.at[r], right_send.at[k], right_recv.at[r], k, c)

    def left_copy(k):
        return remote(chain.at[k], left.at[r], left_send.at[k], left_recv.at[r], k, c)

    def own_left_copy():
        return remote(own.at[0], left.at[r], left_send.at[c], left_recv.at[r], c, c)

    for step in range(1, n):
        right_copy(lax.rem(r + step, n)).start()
    pl.when(off)(lambda: own_left_copy().start())

    def gq_copy(j):
        return remote(gains, gq0.at[c], gq_send.at[j], gq_recv.at[c], r, j)

    def gp_copy(i):
        return remote(gains, gp0.at[c], gp_send.at[i], gp_recv.at[c], i, r)

    for k in range(n):
        pl.when(k != c)(lambda k=k: gq_copy(k).start())
        pl.when(jnp.logical_or(k != r, off))(lambda k=k: gp_copy(k).start())
    gq0[c] = gains[...]

    @pl.when(diag)
    def _():
        gp0[c] = gains[...]

    rows_step = 32
    lane = lax.broadcasted_iota(jnp.int32, (rows_step, block), 1) + c * block
    sub = lax.broadcasted_iota(jnp.int32, (rows_step, block), 0) + r * block

    @pl.loop(0, block // rows_step)
    def _(s):
        rows = pl.ds(pl.multiple_of(s * rows_step, rows_step), rows_step)
        mr = model[0, rows, :].astype(jnp.float32)
        mi = model[1, rows, :].astype(jnp.float32)
        keep = sub + s * rows_step != lane
        power[rows, :] = jnp.where(keep, mr * mr + mi * mi, 0.0)
        vr[rows, :] = jnp.zeros((rows_step, block), jnp.float32)
        vi[rows, :] = jnp.zeros((rows_step, block), jnp.float32)

    def local_left(src, sem):
        copy = pltpu.make_async_copy(src, left.at[r], sem)
        copy.start()
        copy.wait()

    def arrived(k, onward):
        landed(chain.at[k], chain_recv.at[k])
        copy = remote(chain.at[k], chain.at[k], fwd_send.at[k], chain_recv.at[k], r, c + onward)
        pl.when(jnp.logical_and(c + onward >= 0, c + onward < n))(copy.start)
        pl.when(k != r)(lambda: left_copy(k).start())
        pl.when(k == r)(lambda: local_left(chain.at[k], local_sem.at[0]))

    for step in range(1, n):
        pl.when(c >= step)(lambda: arrived(c - step, 1))
        pl.when(c + step < n)(lambda: arrived(c + step, -1))
    pl.when(diag)(lambda: local_left(own.at[0], local_sem.at[0]))
    mine = pltpu.make_async_copy(own.at[jnp.where(r < c, 0, 1)], right.at[r], local_sem.at[1])
    mine.start()
    mine.wait()

    tile = min(256, block)

    def multiply(a_ref, b_ref, k):
        @pl.loop(0, block // tile)
        def _(s):
            rows = pl.ds(pl.multiple_of(s * tile, tile), tile)
            a = a_ref[k, rows, :]
            b = b_ref[k]
            dot = functools.partial(
                lax.dot_general, dimension_numbers=CONTRACT_LAST, preferred_element_type=jnp.float32
            )
            vr[rows, :] += dot(a, b)
            vi[rows, :] += dot(a[:, half:], b[:, :half]) - dot(a[:, :half], b[:, half:])

    @pl.loop(0, n)
    def _(step):
        k = lax.rem(r + step, n)

        @pl.when(step > 0)
        def _():
            landed(left.at[k], left_recv.at[k])
            landed(right.at[k], right_recv.at[k])

        pl.when(off)(lambda: multiply(left, right, k))

        @pl.when(diag)
        def _():
            multiply(left, left, k)
            multiply(right, right, k)

    @pl.loop(0, block // rows_step)
    def _(s):
        rows = pl.ds(pl.multiple_of(s * rows_step, rows_step), rows_step)
        mr = model[0, rows, :].astype(jnp.float32)
        mi = model[1, rows, :].astype(jnp.float32)
        keep = sub + s * rows_step != lane
        a, b = vr[rows, :], vi[rows, :]
        vr[rows, :] = jnp.where(keep, a * mr + b * mi, 0.0)
        vi[rows, :] = jnp.where(keep, a * mi - b * mr, 0.0)

    for k in range(n):
        pl.when(k != c)(lambda k=k: landed(gq0.at[k], gq_recv.at[k]))
        pl.when(jnp.logical_or(k != c, off))(lambda k=k: landed(gp0.at[k], gp_recv.at[k]))

    def start_gains(ref):
        return [jnp.concatenate([ref[k, part : part + 1, :] for k in range(n)], axis=1) for part in range(2)]

    gp = start_gains(gp0)
    gq = start_gains(gq0)
    lanes = 128
    tiles = block // lanes

    for it in range(ITERS):
        gpr = jnp.broadcast_to(gp[0], (8, block))
        gpi = jnp.broadcast_to(gp[1], (8, block))
        qr[...] = jnp.broadcast_to(gq[0], (lanes, block)).T
        qi[...] = jnp.broadcast_to(gq[1], (lanes, block)).T

        def fold(x):
            total = x[:, :lanes]
            for t in range(1, tiles):
                total = total + x[:, t * lanes : (t + 1) * lanes]
            return total

        def sums(s, carry):
            sum_r, sum_i, sum_e = carry
            rows = pl.ds(pl.multiple_of(s * 8, 8), 8)
            wr, wi = vr[rows, :], vi[rows, :]
            ar, ai = qr[rows, :], qi[rows, :]
            norm = ar * ar + ai * ai
            wide = lambda x: jnp.concatenate([x] * tiles, axis=1)
            ar, ai, norm = wide(ar), wide(ai), wide(norm)
            tr[rows, :] = fold(wr * gpr + wi * gpi)
            ti[rows, :] = fold(wr * gpi - wi * gpr)
            return (
                sum_r + (wr * ar - wi * ai),
                sum_i + (wr * ai + wi * ar),
                sum_e + power[rows, :] * norm,
            )

        zero = jnp.zeros((8, block), jnp.float32)
        sum_r, sum_i, sum_e = lax.fori_loop(0, block // 8, sums, (zero, zero, zero))
        for part, value in enumerate((sum_r, sum_i, sum_e)):
            abuf[it, part : part + 1, :] = jnp.sum(value, axis=0, keepdims=True)
        for part, ref in enumerate((tr, ti)):
            bbuf[it, part : part + 1, :] = jnp.sum(ref[...].T, axis=0, keepdims=True)

        a_copy = remote(abuf.at[it], ain.at[it, r], a_send.at[it], a_recv.at[it, r], c, c)
        b_copy = remote(bbuf.at[it], bin_.at[it, c], b_send.at[it], b_recv.at[it, c], r, r)

        @pl.when(off)
        def _():
            a_copy.start()
            b_copy.start()

        def p_copy(i):
            return remote(gin.at[it, 0], gin.at[it, 0], g_send.at[it, 0, i], g_recv.at[it, 0], i, c)

        def q_copy(j):
            return remote(gin.at[it, 0], gin.at[it, 1], g_send.at[it, 1, j], g_recv.at[it, 1], r, j)

        @pl.when(diag)
        def _():
            total = abuf[it]
            for k in range(n):
                @pl.when(k != r)
                def _():
                    landed(ain.at[it, k], a_recv.at[it, k])
                    landed(bin_.at[it, k], b_recv.at[it, k])

            ain[it, r] = jnp.zeros_like(total)
            bin_[it, r] = jnp.zeros_like(total)
            for k in range(n):
                total = total + ain[it, k]
            extra = bin_[it, 0]
            for k in range(1, n):
                extra = extra + bin_[it, k]
            for part in range(2):
                fresh = (total[part : part + 1] + extra[part : part + 1]) / total[2:3]
                if it == 1:
                    fresh = 0.5 * (fresh + gin[0, 0, part : part + 1, :])
                gin[it, 0, part : part + 1, :] = fresh
                gin[it, 1, part : part + 1, :] = fresh
            for k in range(n):
                @pl.when(k != r)
                def _():
                    q_copy(k).start()
                    if it < ITERS - 1:
                        p_copy(k).start()

        @pl.when(off)
        def _():
            landed(gin.at[it, 1], g_recv.at[it, 1])
            if it < ITERS - 1:
                landed(gin.at[it, 0], g_recv.at[it, 0])

        gp = [gin[it, 0, part : part + 1, :] for part in range(2)]
        gq = [gin[it, 1, part : part + 1, :] for part in range(2)]

    out[...] = gin[ITERS - 1, 1, 0:2, pl.ds(pl.multiple_of(c * share, share), share)]

    pl.when(c < n - 1)(up.wait_send)
    pl.when(c > 0)(down.wait_send)
    for step in range(1, n):
        right_copy(lax.rem(r + step, n)).wait_send()
    pl.when(off)(lambda: own_left_copy().wait_send())

    def gone(k, onward):
        copy = remote(chain.at[k], chain.at[k], fwd_send.at[k], chain_recv.at[k], r, c + onward)
        pl.when(jnp.logical_and(c + onward >= 0, c + onward < n))(copy.wait_send)
        pl.when(k != r)(lambda: left_copy(k).wait_send())

    for step in range(1, n):
        pl.when(c >= step)(lambda: gone(c - step, 1))
        pl.when(c + step < n)(lambda: gone(c + step, -1))
    for k in range(n):
        pl.when(k != c)(lambda k=k: gq_copy(k).wait_send())
        pl.when(jnp.logical_or(k != r, off))(lambda k=k: gp_copy(k).wait_send())
    for it in range(ITERS):
        a_copy = remote(abuf.at[it], ain.at[it, r], a_send.at[it], a_recv.at[it, r], c, c)
        b_copy = remote(bbuf.at[it], bin_.at[it, c], b_send.at[it], b_recv.at[it, c], r, r)

        @pl.when(off)
        def _():
            a_copy.wait_send()
            b_copy.wait_send()

        for k in range(n):
            @pl.when(jnp.logical_and(diag, k != r))
            def _():
                remote(gin.at[it, 0], gin.at[it, 1], g_send.at[it, 1, k], g_recv.at[it, 1], r, k).wait_send()
                if it < ITERS - 1:
                    remote(gin.at[it, 0], gin.at[it, 0], g_send.at[it, 0, k], g_recv.at[it, 0], k, c).wait_send()


def square_body(n, samples, sky_model, initial_gains):
    block, _, times = samples.shape
    half = times // 2
    halves = samples.reshape(block, 2, 2, half).transpose(2, 0, 1, 3).reshape(2, block, 2 * half)
    model = sky_model.transpose(1, 0, 2)
    share = initial_gains.shape[1]
    dma = pltpu.SemaphoreType.DMA
    vmem = pltpu.VMEM
    f32, bf16 = jnp.float32, jnp.bfloat16
    piece = (n, block, 2 * half)
    return pl.pallas_call(
        functools.partial(calibrate, n),
        out_shape=jax.ShapeDtypeStruct((2, share), f32),
        in_specs=[pl.BlockSpec(memory_space=pltpu.VMEM)] * 3,
        out_specs=pl.BlockSpec(memory_space=pltpu.VMEM),
        scratch_shapes=[
            vmem(piece, bf16),
            vmem(piece, bf16),
            vmem(piece, bf16),
            vmem((block, block), f32),
            vmem((block, block), f32),
            vmem((block, block), f32),
            vmem((block, 128), f32),
            vmem((block, 128), f32),
            vmem((block, 128), f32),
            vmem((block, 128), f32),
            vmem((n, 2, share), f32),
            vmem((n, 2, share), f32),
            vmem((ITERS, 8, block), f32),
            vmem((ITERS, 8, block), f32),
            vmem((ITERS, n, 8, block), f32),
            vmem((ITERS, n, 8, block), f32),
            vmem((ITERS, 2, 8, block), f32),
            dma((2,)), dma((n,)), dma((n,)),
            dma((n,)), dma((n,)), dma((n,)), dma((n,)), dma((2,)),
            dma((n,)), dma((n,)), dma((n,)), dma((n,)),
            dma((ITERS,)), dma((ITERS, n)), dma((ITERS,)), dma((ITERS, n)),
            dma((ITERS, 2, n)), dma((ITERS, 2)),
        ],
        compiler_params=pltpu.CompilerParams(
            collective_id=0, has_side_effects=True, vmem_limit_bytes=56 * 1024 * 1024
        ),
        cost_estimate=pl.CostEstimate(
            flops=8 * block * block * times * n // 2, bytes_accessed=8 * block * block, transcendentals=0
        ),
    )(halves, model, initial_gains)


def body(samples, sky_model, initial_gains):
    row_count = lax.axis_size("row")
    column_count = lax.axis_size("col")
    row_index = lax.axis_index("row")
    column_index = lax.axis_index("col")
    block_column = samples.shape[0]
    block_row = sky_model.shape[0]
    share_size = initial_gains.shape[1]
    contract_last = (((1,), (1,)), ((), ()))
    upper_limit = lax.Precision.HIGHEST
    own_start = (row_index * column_count + column_index) * share_size
    flattened = samples.reshape(block_column, -1)
    rotated = jnp.concatenate([-samples[:, 1, :], samples[:, 0, :]], axis=1)
    right_side = jnp.concatenate([flattened, rotated], axis=0)
    all_antennas = lax.all_gather(flattened, "col", axis=0, tiled=True)
    vis_tile = lax.psum_scatter(
        lax.dot_general(
            all_antennas, right_side, contract_last, preferred_element_type=jnp.float32
        ),
        "row",
        scatter_dimension=0,
        tiled=True,
    )
    vis_real = vis_tile[:, :block_column]
    vis_imag = vis_tile[:, block_column:]
    model_real = sky_model[:, 0, :].astype(jnp.float32)
    model_imag = sky_model[:, 1, :].astype(jnp.float32)
    global_rows = row_index * block_row + lax.broadcasted_iota(
        jnp.int32, (block_row, block_column), 0
    )
    global_columns = column_index * block_column + lax.broadcasted_iota(
        jnp.int32, (block_row, block_column), 1
    )
    cross_mask = (global_rows != global_columns).astype(jnp.float32)
    weight_real = (vis_real * model_real + vis_imag * model_imag) * cross_mask
    weight_imag = (vis_real * model_imag - vis_imag * model_real) * cross_mask
    model_power = (model_real * model_real + model_imag * model_imag) * cross_mask
    stacked = jnp.concatenate([weight_real, weight_imag], axis=0)
    row_gains = lax.all_gather(initial_gains, "col", axis=1, tiled=True)
    everything = row_gains
    for iteration in range(ITERS):
        gain_real = row_gains[0]
        gain_imag = row_gains[1]
        left_rows = jnp.stack(
            [jnp.concatenate([gain_real, -gain_imag]), jnp.concatenate([gain_imag, gain_real])]
        )
        totals = jnp.dot(left_rows, stacked, precision=upper_limit)
        energy = jnp.dot(
            gain_real * gain_real + gain_imag * gain_imag, model_power, precision=upper_limit
        )
        totals, energy = (totals, energy)
        totals, energy = (
            lax.psum_scatter(totals, "row", scatter_dimension=1, tiled=True),
            lax.psum_scatter(energy, "row", scatter_dimension=0, tiled=True),
        )
        updated = totals / energy[None, :]
        if iteration == 1:
            previous = lax.dynamic_slice_in_dim(
                everything, (column_index * row_count + row_index) * share_size, share_size, 1
            )
            updated = 0.5 * (updated + previous)
        gain_block = lax.all_gather(updated, "row", axis=1, tiled=True)
        everything = lax.all_gather(gain_block, "col", axis=1, tiled=True)
        row_gains = lax.dynamic_slice_in_dim(everything, row_index * block_row, block_row, 1)
    return lax.dynamic_slice_in_dim(everything, own_start, share_size, 1)


def solution(mesh):
    n = mesh.shape["row"]
    square = n == mesh.shape["col"]
    return jax.shard_map(
        functools.partial(square_body, n) if square else body,
        mesh=mesh,
        in_specs=(
            P(("chan", "col"), None, "row"),
            P(("chan", "row"), None, "col"),
            P(None, ("chan", "row", "col")),
        ),
        out_specs=P(None, ("chan", "row", "col")),
        check_vma=False,
    )
```

```python
import functools

import jax
import jax.numpy as jnp
from jax import lax
from jax.experimental import pallas as pl
from jax.experimental.pallas import tpu as pltpu
from jax.sharding import PartitionSpec as P

ITERS = 3
MESH = pl.DeviceIdType.MESH
CONTRACT_LAST = (((1,), (1,)), ((), ()))


def remote(src, dst, send, recv, row, col):
    return pltpu.make_async_remote_copy(
        src_ref=src,
        dst_ref=dst,
        send_sem=send,
        recv_sem=recv,
        device_id={"row": row, "col": col},
        device_id_type=MESH,
    )


def landed(ref, sem):
    pltpu.make_async_copy(ref, ref, sem).wait()


def calibrate(
    n, own, sky, gains, out, chain, left, right, vr, vi, power, model, qr, qi, tr, ti, gp0, gq0,
    abuf, bbuf, ain, bin_, gin,
    up_send, fwd_send, chain_recv, left_send, left_recv, right_send, right_recv, local_sem,
    gp_send, gp_recv, gq_send, gq_recv, a_send, a_recv, b_send, b_recv, g_send, g_recv,
):
    r = lax.axis_index("row")
    c = lax.axis_index("col")
    block = own.shape[1]
    half = own.shape[2] // 2
    share = gains.shape[1]

    def mine_at(h):
        return own.at[:, :, pl.ds(pl.multiple_of(h * half, half), half)]

    diag = r == c
    off = r != c

    barrier = pltpu.get_barrier_semaphore()
    for step in range(1, n * n):
        other = lax.rem(r * n + c + step, n * n)
        pl.semaphore_signal(
            barrier, inc=1, device_id={"row": other // n, "col": lax.rem(other, n)}, device_id_type=MESH
        )
    pl.semaphore_wait(barrier, n * n - 1)

    up = remote(mine_at(0), chain.at[c], up_send.at[0], chain_recv.at[c], r, c + 1)
    down = remote(mine_at(1), chain.at[c], up_send.at[1], chain_recv.at[c], r, c - 1)
    pl.when(c < n - 1)(up.start)
    pl.when(c > 0)(down.start)

    def right_copy(k):
        h = jnp.where(k < c, 0, 1)
        return remote(mine_at(h), right.at[r], right_send.at[k], right_recv.at[r], k, c)

    def left_copy(k):
        return remote(chain.at[k], left.at[r], left_send.at[k], left_recv.at[r], k, c)

    def own_left_copy():
        return remote(mine_at(0), left.at[r], left_send.at[c], left_recv.at[r], c, c)

    for step in range(1, n):
        right_copy(lax.rem(r + step, n)).start()
    pl.when(off)(lambda: own_left_copy().start())

    def gq_copy(j):
        return remote(gains, gq0.at[c], gq_send.at[j], gq_recv.at[c], r, j)

    def gp_copy(i):
        return remote(gains, gp0.at[c], gp_send.at[i], gp_recv.at[c], i, r)

    for k in range(n):
        pl.when(k != c)(lambda k=k: gq_copy(k).start())
        pl.when(jnp.logical_or(k != r, off))(lambda k=k: gp_copy(k).start())
    gq0[c] = gains[...]

    @pl.when(diag)
    def _():
        gp0[c] = gains[...]

    rows_step = 32
    lane = lax.broadcasted_iota(jnp.int32, (rows_step, block), 1) + c * block
    sub = lax.broadcasted_iota(jnp.int32, (rows_step, block), 0) + r * block

    @pl.loop(0, block // rows_step)
    def _(s):
        rows = pl.ds(pl.multiple_of(s * rows_step, rows_step), rows_step)
        pair = sky[rows].astype(jnp.float32)
        mr, mi = pair[:, 0, :], pair[:, 1, :]
        keep = sub + s * rows_step != lane
        mr = jnp.where(keep, mr, 0.0)
        mi = jnp.where(keep, mi, 0.0)
        model[0, rows, :] = mr
        model[1, rows, :] = mi
        power[rows, :] = mr * mr + mi * mi
        vr[rows, :] = jnp.zeros((rows_step, block), jnp.float32)
        vi[rows, :] = jnp.zeros((rows_step, block), jnp.float32)

    def local_left(src, sem):
        copy = pltpu.make_async_copy(src, left.at[r], sem)
        copy.start()
        copy.wait()

    def arrived(k, onward):
        landed(chain.at[k], chain_recv.at[k])
        copy = remote(chain.at[k], chain.at[k], fwd_send.at[k], chain_recv.at[k], r, c + onward)
        pl.when(jnp.logical_and(c + onward >= 0, c + onward < n))(copy.start)
        pl.when(k != r)(lambda: left_copy(k).start())
        pl.when(k == r)(lambda: local_left(chain.at[k], local_sem.at[0]))

    for step in range(1, n):
        pl.when(c >= step)(lambda: arrived(c - step, 1))
        pl.when(c + step < n)(lambda: arrived(c + step, -1))
    pl.when(diag)(lambda: local_left(mine_at(0), local_sem.at[0]))
    mine = pltpu.make_async_copy(mine_at(jnp.where(r < c, 0, 1)), right.at[r], local_sem.at[1])
    mine.start()
    mine.wait()

    tile = min(256, block)

    def multiply(a_ref, b_ref, k):
        @pl.loop(0, block // tile)
        def _(s):
            rows = pl.ds(pl.multiple_of(s * tile, tile), tile)
            ar, ai = a_ref[k, 0, rows, :], a_ref[k, 1, rows, :]
            br, bi = b_ref[k, 0], b_ref[k, 1]
            dot = functools.partial(
                lax.dot_general, dimension_numbers=CONTRACT_LAST, preferred_element_type=jnp.float32
            )
            both = lambda x, y: jnp.concatenate([x, y], axis=1)
            vr[rows, :] += dot(both(ar, ai), both(br, bi))
            vi[rows, :] += dot(both(ai, -ar), both(br, bi))

    @pl.loop(0, n)
    def _(step):
        k = lax.rem(r + step, n)

        @pl.when(step > 0)
        def _():
            landed(left.at[k], left_recv.at[k])
            landed(right.at[k], right_recv.at[k])

        pl.when(off)(lambda: multiply(left, right, k))

        @pl.when(diag)
        def _():
            multiply(left, left, k)
            multiply(right, right, k)

    @pl.loop(0, block // rows_step)
    def _(s):
        rows = pl.ds(pl.multiple_of(s * rows_step, rows_step), rows_step)
        mr, mi = model[0, rows, :], model[1, rows, :]
        a, b = vr[rows, :], vi[rows, :]
        vr[rows, :] = a * mr + b * mi
        vi[rows, :] = a * mi - b * mr

    for k in range(n):
        pl.when(k != c)(lambda k=k: landed(gq0.at[k], gq_recv.at[k]))
        pl.when(jnp.logical_or(k != c, off))(lambda k=k: landed(gp0.at[k], gp_recv.at[k]))

    def start_gains(ref):
        return [jnp.concatenate([ref[k, part : part + 1, :] for k in range(n)], axis=1) for part in range(2)]

    gp = start_gains(gp0)
    gq = start_gains(gq0)
    lanes = 128
    tiles = block // lanes

    for it in range(ITERS):
        gpr = jnp.broadcast_to(gp[0], (8, block))
        gpi = jnp.broadcast_to(gp[1], (8, block))
        qr[...] = jnp.broadcast_to(gq[0], (lanes, block)).T
        qi[...] = jnp.broadcast_to(gq[1], (lanes, block)).T

        def fold(x):
            total = x[:, :lanes]
            for t in range(1, tiles):
                total = total + x[:, t * lanes : (t + 1) * lanes]
            return total

        def sums(s, carry):
            sum_r, sum_i, sum_e = carry
            rows = pl.ds(pl.multiple_of(s * 8, 8), 8)
            wr, wi = vr[rows, :], vi[rows, :]
            ar, ai = qr[rows, :], qi[rows, :]
            norm = ar * ar + ai * ai
            wide = lambda x: jnp.concatenate([x] * tiles, axis=1)
            ar, ai, norm = wide(ar), wide(ai), wide(norm)
            tr[rows, :] = fold(wr * gpr + wi * gpi)
            ti[rows, :] = fold(wr * gpi - wi * gpr)
            return (
                sum_r + (wr * ar - wi * ai),
                sum_i + (wr * ai + wi * ar),
                sum_e + power[rows, :] * norm,
            )

        zero = jnp.zeros((8, block), jnp.float32)
        sum_r, sum_i, sum_e = lax.fori_loop(0, block // 8, sums, (zero, zero, zero))
        for part, value in enumerate((sum_r, sum_i, sum_e)):
            abuf[it, part : part + 1, :] = jnp.sum(value, axis=0, keepdims=True)
        for part, ref in enumerate((tr, ti)):
            bbuf[it, part : part + 1, :] = jnp.sum(ref[...].T, axis=0, keepdims=True)

        a_copy = remote(abuf.at[it], ain.at[it, r], a_send.at[it], a_recv.at[it, r], c, c)
        b_copy = remote(bbuf.at[it], bin_.at[it, c], b_send.at[it], b_recv.at[it, c], r, r)

        @pl.when(off)
        def _():
            a_copy.start()
            b_copy.start()

        def p_copy(i):
            return remote(gin.at[it, 0], gin.at[it, 0], g_send.at[it, 0, i], g_recv.at[it, 0], i, c)

        def q_copy(j):
            return remote(gin.at[it, 0], gin.at[it, 1], g_send.at[it, 1, j], g_recv.at[it, 1], r, j)

        @pl.when(diag)
        def _():
            total = abuf[it]
            for k in range(n):
                @pl.when(k != r)
                def _():
                    landed(ain.at[it, k], a_recv.at[it, k])
                    landed(bin_.at[it, k], b_recv.at[it, k])

            ain[it, r] = jnp.zeros_like(total)
            bin_[it, r] = jnp.zeros((2, block), jnp.float32)
            for k in range(n):
                total = total + ain[it, k]
            extra = bin_[it, 0]
            for k in range(1, n):
                extra = extra + bin_[it, k]
            for part in range(2):
                fresh = (total[part : part + 1] + extra[part : part + 1]) / total[2:3]
                if it == 1:
                    fresh = 0.5 * (fresh + gin[0, 0, part : part + 1, :])
                gin[it, 0, part : part + 1, :] = fresh
                gin[it, 1, part : part + 1, :] = fresh
            for k in range(n):
                @pl.when(k != r)
                def _():
                    q_copy(k).start()
                    if it < ITERS - 1:
                        p_copy(k).start()

        @pl.when(off)
        def _():
            landed(gin.at[it, 1], g_recv.at[it, 1])
            if it < ITERS - 1:
                landed(gin.at[it, 0], g_recv.at[it, 0])

        gp = [gin[it, 0, part : part + 1, :] for part in range(2)]
        gq = [gin[it, 1, part : part + 1, :] for part in range(2)]

    out[...] = gin[ITERS - 1, 1, 0:2, pl.ds(pl.multiple_of(c * share, share), share)]

    pl.when(c < n - 1)(up.wait_send)
    pl.when(c > 0)(down.wait_send)
    for step in range(1, n):
        right_copy(lax.rem(r + step, n)).wait_send()
    pl.when(off)(lambda: own_left_copy().wait_send())

    def gone(k, onward):
        copy = remote(chain.at[k], chain.at[k], fwd_send.at[k], chain_recv.at[k], r, c + onward)
        pl.when(jnp.logical_and(c + onward >= 0, c + onward < n))(copy.wait_send)
        pl.when(k != r)(lambda: left_copy(k).wait_send())

    for step in range(1, n):
        pl.when(c >= step)(lambda: gone(c - step, 1))
        pl.when(c + step < n)(lambda: gone(c + step, -1))
    for k in range(n):
        pl.when(k != c)(lambda k=k: gq_copy(k).wait_send())
        pl.when(jnp.logical_or(k != r, off))(lambda k=k: gp_copy(k).wait_send())
    for it in range(ITERS):
        a_copy = remote(abuf.at[it], ain.at[it, r], a_send.at[it], a_recv.at[it, r], c, c)
        b_copy = remote(bbuf.at[it], bin_.at[it, c], b_send.at[it], b_recv.at[it, c], r, r)

        @pl.when(off)
        def _():
            a_copy.wait_send()
            b_copy.wait_send()

        for k in range(n):
            @pl.when(jnp.logical_and(diag, k != r))
            def _():
                remote(gin.at[it, 0], gin.at[it, 1], g_send.at[it, 1, k], g_recv.at[it, 1], r, k).wait_send()
                if it < ITERS - 1:
                    remote(gin.at[it, 0], gin.at[it, 0], g_send.at[it, 0, k], g_recv.at[it, 0], k, c).wait_send()


def square_body(n, samples, sky_model, initial_gains):
    block, _, times = samples.shape
    half = times // 2
    parts = samples.transpose(1, 0, 2)
    share = initial_gains.shape[1]
    dma = pltpu.SemaphoreType.DMA
    vmem = pltpu.VMEM
    f32, bf16 = jnp.float32, jnp.bfloat16
    piece = (n, 2, block, half)
    return pl.pallas_call(
        functools.partial(calibrate, n),
        out_shape=jax.ShapeDtypeStruct((2, share), f32),
        in_specs=[pl.BlockSpec(memory_space=pltpu.VMEM)] * 3,
        out_specs=pl.BlockSpec(memory_space=pltpu.VMEM),
        scratch_shapes=[
            vmem(piece, bf16),
            vmem(piece, bf16),
            vmem(piece, bf16),
            vmem((block, block), f32),
            vmem((block, block), f32),
            vmem((block, block), f32),
            vmem((2, block, block), f32),
            vmem((block, 128), f32),
            vmem((block, 128), f32),
            vmem((block, 128), f32),
            vmem((block, 128), f32),
            vmem((n, 2, share), f32),
            vmem((n, 2, share), f32),
            vmem((ITERS, 4, block), f32),
            vmem((ITERS, 2, block), f32),
            vmem((ITERS, n, 4, block), f32),
            vmem((ITERS, n, 2, block), f32),
            vmem((ITERS, 2, 2, block), f32),
            dma((2,)), dma((n,)), dma((n,)),
            dma((n,)), dma((n,)), dma((n,)), dma((n,)), dma((2,)),
            dma((n,)), dma((n,)), dma((n,)), dma((n,)),
            dma((ITERS,)), dma((ITERS, n)), dma((ITERS,)), dma((ITERS, n)),
            dma((ITERS, 2, n)), dma((ITERS, 2)),
        ],
        compiler_params=pltpu.CompilerParams(
            collective_id=0, has_side_effects=True, vmem_limit_bytes=56 * 1024 * 1024
        ),
        cost_estimate=pl.CostEstimate(
            flops=8 * block * block * times * n // 2, bytes_accessed=8 * block * block, transcendentals=0
        ),
    )(parts, sky_model, initial_gains)


def body(samples, sky_model, initial_gains):
    row_count = lax.axis_size("row")
    column_count = lax.axis_size("col")
    row_index = lax.axis_index("row")
    column_index = lax.axis_index("col")
    block_column = samples.shape[0]
    block_row = sky_model.shape[0]
    share_size = initial_gains.shape[1]
    contract_last = (((1,), (1,)), ((), ()))
    upper_limit = lax.Precision.HIGHEST
    own_start = (row_index * column_count + column_index) * share_size
    flattened = samples.reshape(block_column, -1)
    rotated = jnp.concatenate([-samples[:, 1, :], samples[:, 0, :]], axis=1)
    right_side = jnp.concatenate([flattened, rotated], axis=0)
    all_antennas = lax.all_gather(flattened, "col", axis=0, tiled=True)
    vis_tile = lax.psum_scatter(
        lax.dot_general(
            all_antennas, right_side, contract_last, preferred_element_type=jnp.float32
        ),
        "row",
        scatter_dimension=0,
        tiled=True,
    )
    vis_real = vis_tile[:, :block_column]
    vis_imag = vis_tile[:, block_column:]
    model_real = sky_model[:, 0, :].astype(jnp.float32)
    model_imag = sky_model[:, 1, :].astype(jnp.float32)
    global_rows = row_index * block_row + lax.broadcasted_iota(
        jnp.int32, (block_row, block_column), 0
    )
    global_columns = column_index * block_column + lax.broadcasted_iota(
        jnp.int32, (block_row, block_column), 1
    )
    cross_mask = (global_rows != global_columns).astype(jnp.float32)
    weight_real = (vis_real * model_real + vis_imag * model_imag) * cross_mask
    weight_imag = (vis_real * model_imag - vis_imag * model_real) * cross_mask
    model_power = (model_real * model_real + model_imag * model_imag) * cross_mask
    stacked = jnp.concatenate([weight_real, weight_imag], axis=0)
    row_gains = lax.all_gather(initial_gains, "col", axis=1, tiled=True)
    everything = row_gains
    for iteration in range(ITERS):
        gain_real = row_gains[0]
        gain_imag = row_gains[1]
        left_rows = jnp.stack(
            [jnp.concatenate([gain_real, -gain_imag]), jnp.concatenate([gain_imag, gain_real])]
        )
        totals = jnp.dot(left_rows, stacked, precision=upper_limit)
        energy = jnp.dot(
            gain_real * gain_real + gain_imag * gain_imag, model_power, precision=upper_limit
        )
        totals, energy = (totals, energy)
        totals, energy = (
            lax.psum_scatter(totals, "row", scatter_dimension=1, tiled=True),
            lax.psum_scatter(energy, "row", scatter_dimension=0, tiled=True),
        )
        updated = totals / energy[None, :]
        if iteration == 1:
            previous = lax.dynamic_slice_in_dim(
                everything, (column_index * row_count + row_index) * share_size, share_size, 1
            )
            updated = 0.5 * (updated + previous)
        gain_block = lax.all_gather(updated, "row", axis=1, tiled=True)
        everything = lax.all_gather(gain_block, "col", axis=1, tiled=True)
        row_gains = lax.dynamic_slice_in_dim(everything, row_index * block_row, block_row, 1)
    return lax.dynamic_slice_in_dim(everything, own_start, share_size, 1)


def solution(mesh):
    n = mesh.shape["row"]
    square = n == mesh.shape["col"]
    return jax.shard_map(
        functools.partial(square_body, n) if square else body,
        mesh=mesh,
        in_specs=(
            P(("chan", "col"), None, "row"),
            P(("chan", "row"), None, "col"),
            P(None, ("chan", "row", "col")),
        ),
        out_specs=P(None, ("chan", "row", "col")),
        check_vma=False,
    )
```

```python
import functools

import jax
import jax.numpy as jnp
from jax import lax
from jax.experimental import pallas as pl
from jax.experimental.pallas import tpu as pltpu
from jax.sharding import PartitionSpec as P

ITERS = 3
CHUNKS = 4
MESH = pl.DeviceIdType.MESH
CONTRACT_LAST = (((1,), (1,)), ((), ()))


def remote(src, dst, send, recv, row, col):
    return pltpu.make_async_remote_copy(
        src_ref=src,
        dst_ref=dst,
        send_sem=send,
        recv_sem=recv,
        device_id={"row": row, "col": col},
        device_id_type=MESH,
    )


def landed(ref, sem):
    pltpu.make_async_copy(ref, ref, sem).wait()


def calibrate(
    n, own, sky, gains, out, chain, left, right, vr, vi, power, model, qr, qi, tr, ti, gp0, gq0,
    abuf, bbuf, ain, bin_, gin,
    up_send, fwd_send, chain_recv, left_send, left_recv, right_send, right_recv, local_sem,
    gp_send, gp_recv, gq_send, gq_recv, a_send, a_recv, b_send, b_recv, g_send, g_recv,
):
    r = lax.axis_index("row")
    c = lax.axis_index("col")
    block = own.shape[1]
    half = own.shape[2] // 2
    share = gains.shape[1]

    tile = max(block // CHUNKS, 16)
    chunks = range(block // tile)

    def mine_at(h):
        return own.at[:, :, pl.ds(pl.multiple_of(h * half, half), half)]

    def part_of(ref, k, s):
        return ref.at[k, :, pl.ds(s * tile, tile), :]

    def mine_part(h, s):
        return own.at[:, pl.ds(s * tile, tile), pl.ds(h * half, half)]

    diag = r == c
    off = r != c

    barrier = pltpu.get_barrier_semaphore()
    for step in range(1, n * n):
        other = lax.rem(r * n + c + step, n * n)
        pl.semaphore_signal(
            barrier, inc=1, device_id={"row": other // n, "col": lax.rem(other, n)}, device_id_type=MESH
        )
    pl.semaphore_wait(barrier, n * n - 1)

    def up(s):
        return remote(mine_part(0, s), part_of(chain, c, s), up_send.at[0, s], chain_recv.at[c, s], r, c + 1)

    def down(s):
        return remote(mine_part(1, s), part_of(chain, c, s), up_send.at[1, s], chain_recv.at[c, s], r, c - 1)

    for s in chunks:
        pl.when(c < n - 1)(lambda: up(s).start())
        pl.when(c > 0)(lambda: down(s).start())

    def right_copy(k):
        h = jnp.where(k < c, 0, 1)
        return remote(mine_at(h), right.at[r], right_send.at[k], right_recv.at[r], k, c)

    def left_copy(k, s):
        return remote(
            part_of(chain, k, s), part_of(left, r, s), left_send.at[k, s], left_recv.at[r, s], k, c
        )

    def own_left_copy(s):
        return remote(
            mine_part(0, s), part_of(left, r, s), left_send.at[c, s], left_recv.at[r, s], c, c
        )

    for step in range(1, n):
        right_copy(lax.rem(r + step, n)).start()
    for s in chunks:
        pl.when(off)(lambda: own_left_copy(s).start())

    def gq_copy(j):
        return remote(gains, gq0.at[c], gq_send.at[j], gq_recv.at[c], r, j)

    def gp_copy(i):
        return remote(gains, gp0.at[c], gp_send.at[i], gp_recv.at[c], i, r)

    for k in range(n):
        pl.when(k != c)(lambda k=k: gq_copy(k).start())
        pl.when(jnp.logical_or(k != r, off))(lambda k=k: gp_copy(k).start())
    gq0[c] = gains[...]

    @pl.when(diag)
    def _():
        gp0[c] = gains[...]

    rows_step = 32
    lane = lax.broadcasted_iota(jnp.int32, (rows_step, block), 1) + c * block
    sub = lax.broadcasted_iota(jnp.int32, (rows_step, block), 0) + r * block

    @pl.loop(0, block // rows_step)
    def _(s):
        rows = pl.ds(pl.multiple_of(s * rows_step, rows_step), rows_step)
        pair = sky[rows].astype(jnp.float32)
        mr, mi = pair[:, 0, :], pair[:, 1, :]
        keep = sub + s * rows_step != lane
        mr = jnp.where(keep, mr, 0.0)
        mi = jnp.where(keep, mi, 0.0)
        model[0, rows, :] = mr
        model[1, rows, :] = mi
        power[rows, :] = mr * mr + mi * mi
        vr[rows, :] = jnp.zeros((rows_step, block), jnp.float32)
        vi[rows, :] = jnp.zeros((rows_step, block), jnp.float32)

    mine = pltpu.make_async_copy(mine_at(jnp.where(r < c, 0, 1)), right.at[r], local_sem.at[1])
    mine.start()
    mine.wait()

    def multiply(a_ref, b_ref, k, s):
        rows = pl.ds(pl.multiple_of(s * tile, tile), tile)
        ar, ai = a_ref[k, 0, rows, :], a_ref[k, 1, rows, :]
        br, bi = b_ref[k, 0], b_ref[k, 1]
        dot = functools.partial(
            lax.dot_general, dimension_numbers=CONTRACT_LAST, preferred_element_type=jnp.float32
        )
        both = lambda x, y: jnp.concatenate([x, y], axis=1)
        vr[rows, :] += dot(both(ar, ai), both(br, bi))
        vi[rows, :] += dot(both(ai, -ar), both(br, bi))

    @pl.when(diag)
    def _():
        copy = pltpu.make_async_copy(mine_at(0), left.at[r], local_sem.at[0])
        copy.start()
        copy.wait()

        @pl.loop(0, len(chunks))
        def _(s):
            multiply(left, left, r, s)
            multiply(right, right, r, s)

    def onward_copy(k, s, onward):
        return remote(
            part_of(chain, k, s), part_of(chain, k, s), fwd_send.at[k, s], chain_recv.at[k, s], r, c + onward
        )

    def arrived(k, s, onward):
        landed(part_of(chain, k, s), chain_recv.at[k, s])
        pl.when(jnp.logical_and(c + onward >= 0, c + onward < n))(lambda: onward_copy(k, s, onward).start())
        pl.when(k != r)(lambda: left_copy(k, s).start())

    for step in range(1, n):
        for s in chunks:
            pl.when(c >= step)(lambda: arrived(c - step, s, 1))
            pl.when(c + step < n)(lambda: arrived(c + step, s, -1))

    @pl.when(off)
    def _():
        @pl.loop(0, len(chunks))
        def _(s):
            multiply(chain, right, r, s)

    for step in range(1, n):
        landed(right.at[lax.rem(r + step, n)], right_recv.at[lax.rem(r + step, n)])

    @pl.loop(0, len(chunks))
    def _(s):
        @pl.loop(1, n)
        def _(step):
            k = lax.rem(r + step, n)
            rows = pl.ds(pl.multiple_of(s * tile, tile), tile)
            landed(left.at[k, :, rows, :], left_recv.at[k, s])
            pl.when(off)(lambda: multiply(left, right, k, s))

    @pl.when(diag)
    def _():
        @pl.loop(1, n)
        def _(step):
            k = lax.rem(r + step, n)

            @pl.loop(0, len(chunks))
            def _(s):
                multiply(left, left, k, s)
                multiply(right, right, k, s)

    @pl.loop(0, block // rows_step)
    def _(s):
        rows = pl.ds(pl.multiple_of(s * rows_step, rows_step), rows_step)
        mr, mi = model[0, rows, :], model[1, rows, :]
        a, b = vr[rows, :], vi[rows, :]
        vr[rows, :] = a * mr + b * mi
        vi[rows, :] = a * mi - b * mr

    for k in range(n):
        pl.when(k != c)(lambda k=k: landed(gq0.at[k], gq_recv.at[k]))
        pl.when(jnp.logical_or(k != c, off))(lambda k=k: landed(gp0.at[k], gp_recv.at[k]))

    def start_gains(ref):
        return [jnp.concatenate([ref[k, part : part + 1, :] for k in range(n)], axis=1) for part in range(2)]

    gp = start_gains(gp0)
    gq = start_gains(gq0)
    lanes = 128
    tiles = block // lanes

    for it in range(ITERS):
        gpr = jnp.broadcast_to(gp[0], (8, block))
        gpi = jnp.broadcast_to(gp[1], (8, block))
        qr[...] = jnp.broadcast_to(gq[0], (lanes, block)).T
        qi[...] = jnp.broadcast_to(gq[1], (lanes, block)).T

        def fold(x):
            total = x[:, :lanes]
            for t in range(1, tiles):
                total = total + x[:, t * lanes : (t + 1) * lanes]
            return total

        def sums(s, carry):
            sum_r, sum_i, sum_e = carry
            rows = pl.ds(pl.multiple_of(s * 8, 8), 8)
            wr, wi = vr[rows, :], vi[rows, :]
            ar, ai = qr[rows, :], qi[rows, :]
            norm = ar * ar + ai * ai
            wide = lambda x: jnp.concatenate([x] * tiles, axis=1)
            ar, ai, norm = wide(ar), wide(ai), wide(norm)
            tr[rows, :] = fold(wr * gpr + wi * gpi)
            ti[rows, :] = fold(wr * gpi - wi * gpr)
            return (
                sum_r + (wr * ar - wi * ai),
                sum_i + (wr * ai + wi * ar),
                sum_e + power[rows, :] * norm,
            )

        zero = jnp.zeros((8, block), jnp.float32)
        sum_r, sum_i, sum_e = lax.fori_loop(0, block // 8, sums, (zero, zero, zero))
        for part, value in enumerate((sum_r, sum_i, sum_e)):
            abuf[it, part : part + 1, :] = jnp.sum(value, axis=0, keepdims=True)
        for part, ref in enumerate((tr, ti)):
            bbuf[it, part : part + 1, :] = jnp.sum(ref[...].T, axis=0, keepdims=True)

        a_copy = remote(abuf.at[it], ain.at[it, r], a_send.at[it], a_recv.at[it, r], c, c)
        b_copy = remote(bbuf.at[it], bin_.at[it, c], b_send.at[it], b_recv.at[it, c], r, r)

        @pl.when(off)
        def _():
            a_copy.start()
            b_copy.start()

        def p_copy(i):
            return remote(gin.at[it, 0], gin.at[it, 0], g_send.at[it, 0, i], g_recv.at[it, 0], i, c)

        def q_copy(j):
            return remote(gin.at[it, 0], gin.at[it, 1], g_send.at[it, 1, j], g_recv.at[it, 1], r, j)

        @pl.when(diag)
        def _():
            total = abuf[it]
            for k in range(n):
                @pl.when(k != r)
                def _():
                    landed(ain.at[it, k], a_recv.at[it, k])
                    landed(bin_.at[it, k], b_recv.at[it, k])

            ain[it, r] = jnp.zeros_like(total)
            bin_[it, r] = jnp.zeros((2, block), jnp.float32)
            for k in range(n):
                total = total + ain[it, k]
            extra = bin_[it, 0]
            for k in range(1, n):
                extra = extra + bin_[it, k]
            for part in range(2):
                fresh = (total[part : part + 1] + extra[part : part + 1]) / total[2:3]
                if it == 1:
                    fresh = 0.5 * (fresh + gin[0, 0, part : part + 1, :])
                gin[it, 0, part : part + 1, :] = fresh
                gin[it, 1, part : part + 1, :] = fresh
            for k in range(n):
                @pl.when(k != r)
                def _():
                    q_copy(k).start()
                    if it < ITERS - 1:
                        p_copy(k).start()

        @pl.when(off)
        def _():
            landed(gin.at[it, 1], g_recv.at[it, 1])
            if it < ITERS - 1:
                landed(gin.at[it, 0], g_recv.at[it, 0])

        gp = [gin[it, 0, part : part + 1, :] for part in range(2)]
        gq = [gin[it, 1, part : part + 1, :] for part in range(2)]

    out[...] = gin[ITERS - 1, 1, 0:2, pl.ds(pl.multiple_of(c * share, share), share)]

    for step in range(1, n):
        right_copy(lax.rem(r + step, n)).wait_send()

    def gone(k, s, onward):
        pl.when(jnp.logical_and(c + onward >= 0, c + onward < n))(lambda: onward_copy(k, s, onward).wait_send())
        pl.when(k != r)(lambda: left_copy(k, s).wait_send())

    for s in chunks:
        pl.when(c < n - 1)(lambda: up(s).wait_send())
        pl.when(c > 0)(lambda: down(s).wait_send())
        pl.when(off)(lambda: own_left_copy(s).wait_send())
        for step in range(1, n):
            pl.when(c >= step)(lambda: gone(c - step, s, 1))
            pl.when(c + step < n)(lambda: gone(c + step, s, -1))
    for k in range(n):
        pl.when(k != c)(lambda k=k: gq_copy(k).wait_send())
        pl.when(jnp.logical_or(k != r, off))(lambda k=k: gp_copy(k).wait_send())
    for it in range(ITERS):
        a_copy = remote(abuf.at[it], ain.at[it, r], a_send.at[it], a_recv.at[it, r], c, c)
        b_copy = remote(bbuf.at[it], bin_.at[it, c], b_send.at[it], b_recv.at[it, c], r, r)

        @pl.when(off)
        def _():
            a_copy.wait_send()
            b_copy.wait_send()

        for k in range(n):
            @pl.when(jnp.logical_and(diag, k != r))
            def _():
                remote(gin.at[it, 0], gin.at[it, 1], g_send.at[it, 1, k], g_recv.at[it, 1], r, k).wait_send()
                if it < ITERS - 1:
                    remote(gin.at[it, 0], gin.at[it, 0], g_send.at[it, 0, k], g_recv.at[it, 0], k, c).wait_send()


def square_body(n, samples, sky_model, initial_gains):
    block, _, times = samples.shape
    half = times // 2
    parts = samples.transpose(1, 0, 2)
    share = initial_gains.shape[1]
    dma = pltpu.SemaphoreType.DMA
    vmem = pltpu.VMEM
    f32, bf16 = jnp.float32, jnp.bfloat16
    piece = (n, 2, block, half)
    return pl.pallas_call(
        functools.partial(calibrate, n),
        out_shape=jax.ShapeDtypeStruct((2, share), f32),
        in_specs=[pl.BlockSpec(memory_space=pltpu.VMEM)] * 3,
        out_specs=pl.BlockSpec(memory_space=pltpu.VMEM),
        scratch_shapes=[
            vmem(piece, bf16),
            vmem(piece, bf16),
            vmem(piece, bf16),
            vmem((block, block), f32),
            vmem((block, block), f32),
            vmem((block, block), f32),
            vmem((2, block, block), f32),
            vmem((block, 128), f32),
            vmem((block, 128), f32),
            vmem((block, 128), f32),
            vmem((block, 128), f32),
            vmem((n, 2, share), f32),
            vmem((n, 2, share), f32),
            vmem((ITERS, 4, block), f32),
            vmem((ITERS, 2, block), f32),
            vmem((ITERS, n, 4, block), f32),
            vmem((ITERS, n, 2, block), f32),
            vmem((ITERS, 2, 2, block), f32),
            dma((2, CHUNKS)), dma((n, CHUNKS)), dma((n, CHUNKS)),
            dma((n, CHUNKS)), dma((n, CHUNKS)), dma((n,)), dma((n,)), dma((2,)),
            dma((n,)), dma((n,)), dma((n,)), dma((n,)),
            dma((ITERS,)), dma((ITERS, n)), dma((ITERS,)), dma((ITERS, n)),
            dma((ITERS, 2, n)), dma((ITERS, 2)),
        ],
        compiler_params=pltpu.CompilerParams(
            collective_id=0, has_side_effects=True, vmem_limit_bytes=56 * 1024 * 1024
        ),
        cost_estimate=pl.CostEstimate(
            flops=8 * block * block * times * n // 2, bytes_accessed=8 * block * block, transcendentals=0
        ),
    )(parts, sky_model, initial_gains)


def body(samples, sky_model, initial_gains):
    row_count = lax.axis_size("row")
    column_count = lax.axis_size("col")
    row_index = lax.axis_index("row")
    column_index = lax.axis_index("col")
    block_column = samples.shape[0]
    block_row = sky_model.shape[0]
    share_size = initial_gains.shape[1]
    contract_last = (((1,), (1,)), ((), ()))
    upper_limit = lax.Precision.HIGHEST
    own_start = (row_index * column_count + column_index) * share_size
    flattened = samples.reshape(block_column, -1)
    rotated = jnp.concatenate([-samples[:, 1, :], samples[:, 0, :]], axis=1)
    right_side = jnp.concatenate([flattened, rotated], axis=0)
    all_antennas = lax.all_gather(flattened, "col", axis=0, tiled=True)
    vis_tile = lax.psum_scatter(
        lax.dot_general(
            all_antennas, right_side, contract_last, preferred_element_type=jnp.float32
        ),
        "row",
        scatter_dimension=0,
        tiled=True,
    )
    vis_real = vis_tile[:, :block_column]
    vis_imag = vis_tile[:, block_column:]
    model_real = sky_model[:, 0, :].astype(jnp.float32)
    model_imag = sky_model[:, 1, :].astype(jnp.float32)
    global_rows = row_index * block_row + lax.broadcasted_iota(
        jnp.int32, (block_row, block_column), 0
    )
    global_columns = column_index * block_column + lax.broadcasted_iota(
        jnp.int32, (block_row, block_column), 1
    )
    cross_mask = (global_rows != global_columns).astype(jnp.float32)
    weight_real = (vis_real * model_real + vis_imag * model_imag) * cross_mask
    weight_imag = (vis_real * model_imag - vis_imag * model_real) * cross_mask
    model_power = (model_real * model_real + model_imag * model_imag) * cross_mask
    stacked = jnp.concatenate([weight_real, weight_imag], axis=0)
    row_gains = lax.all_gather(initial_gains, "col", axis=1, tiled=True)
    everything = row_gains
    for iteration in range(ITERS):
        gain_real = row_gains[0]
        gain_imag = row_gains[1]
        left_rows = jnp.stack(
            [jnp.concatenate([gain_real, -gain_imag]), jnp.concatenate([gain_imag, gain_real])]
        )
        totals = jnp.dot(left_rows, stacked, precision=upper_limit)
        energy = jnp.dot(
            gain_real * gain_real + gain_imag * gain_imag, model_power, precision=upper_limit
        )
        totals, energy = (totals, energy)
        totals, energy = (
            lax.psum_scatter(totals, "row", scatter_dimension=1, tiled=True),
            lax.psum_scatter(energy, "row", scatter_dimension=0, tiled=True),
        )
        updated = totals / energy[None, :]
        if iteration == 1:
            previous = lax.dynamic_slice_in_dim(
                everything, (column_index * row_count + row_index) * share_size, share_size, 1
            )
            updated = 0.5 * (updated + previous)
        gain_block = lax.all_gather(updated, "row", axis=1, tiled=True)
        everything = lax.all_gather(gain_block, "col", axis=1, tiled=True)
        row_gains = lax.dynamic_slice_in_dim(everything, row_index * block_row, block_row, 1)
    return lax.dynamic_slice_in_dim(everything, own_start, share_size, 1)


def solution(mesh):
    n = mesh.shape["row"]
    square = n == mesh.shape["col"]
    return jax.shard_map(
        functools.partial(square_body, n) if square else body,
        mesh=mesh,
        in_specs=(
            P(("chan", "col"), None, "row"),
            P(("chan", "row"), None, "col"),
            P(None, ("chan", "row", "col")),
        ),
        out_specs=P(None, ("chan", "row", "col")),
        check_vma=False,
    )
```

```python
import functools

import jax
import jax.numpy as jnp
from jax import lax
from jax.experimental import pallas as pl
from jax.experimental.pallas import tpu as pltpu
from jax.sharding import PartitionSpec as P

ITERS = 3
CHUNKS = 4
MESH = pl.DeviceIdType.MESH
CONTRACT_LAST = (((1,), (1,)), ((), ()))


def remote(src, dst, send, recv, row, col):
    return pltpu.make_async_remote_copy(
        src_ref=src,
        dst_ref=dst,
        send_sem=send,
        recv_sem=recv,
        device_id={"row": row, "col": col},
        device_id_type=MESH,
    )


def landed(ref, sem):
    pltpu.make_async_copy(ref, ref, sem).wait()


def calibrate(
    n, own, sky, gains, out, chain, left, right, vr, vi, power, model, qr, qi, tr, ti, gp0, gq0,
    abuf, bbuf, ain, bin_, gin,
    up_send, fwd_send, chain_recv, left_send, left_recv, right_send, right_recv, local_sem,
    gp_send, gp_recv, gq_send, gq_recv, a_send, a_recv, b_send, b_recv, g_send, g_recv,
):
    r = lax.axis_index("row")
    c = lax.axis_index("col")
    block = own.shape[1]
    half = own.shape[2] // 2
    share = gains.shape[1]

    tile = max(block // CHUNKS, 16)
    chunks = range(block // tile)

    def mine_at(h):
        return own.at[:, :, pl.ds(pl.multiple_of(h * half, half), half)]

    def part_of(ref, k, s):
        return ref.at[k, :, pl.ds(s * tile, tile), :]

    def mine_part(h, s):
        return own.at[:, pl.ds(s * tile, tile), pl.ds(h * half, half)]

    diag = r == c
    off = r != c

    barrier = pltpu.get_barrier_semaphore()
    for step in range(1, n * n):
        other = lax.rem(r * n + c + step, n * n)
        pl.semaphore_signal(
            barrier, inc=1, device_id={"row": other // n, "col": lax.rem(other, n)}, device_id_type=MESH
        )
    pl.semaphore_wait(barrier, n * n - 1)

    def up(s):
        return remote(mine_part(0, s), part_of(chain, c, s), up_send.at[0, s], chain_recv.at[c, s], r, c + 1)

    def down(s):
        return remote(mine_part(1, s), part_of(chain, c, s), up_send.at[1, s], chain_recv.at[c, s], r, c - 1)

    ahead = 2
    for s in chunks:
        first = s < ahead
        pl.when(c < n - 1 if first else c == 0)(lambda: up(s).start())
        pl.when(c > 0 if first else c == n - 1)(lambda: down(s).start())

    def right_copy(k):
        h = jnp.where(k < c, 0, 1)
        return remote(mine_at(h), right.at[r], right_send.at[k], right_recv.at[r], k, c)

    def left_copy(k, s):
        return remote(
            part_of(chain, k, s), part_of(left, r, s), left_send.at[k, s], left_recv.at[r, s], k, c
        )

    def own_left_copy(s):
        return remote(
            mine_part(0, s), part_of(left, r, s), left_send.at[c, s], left_recv.at[r, s], c, c
        )

    for step in range(1, n):
        right_copy(lax.rem(r + step, n)).start()
    for s in chunks:
        pl.when(off)(lambda: own_left_copy(s).start())

    def gq_copy(j):
        return remote(gains, gq0.at[c], gq_send.at[j], gq_recv.at[c], r, j)

    def gp_copy(i):
        return remote(gains, gp0.at[c], gp_send.at[i], gp_recv.at[c], i, r)

    for k in range(n):
        pl.when(k != c)(lambda k=k: gq_copy(k).start())
        pl.when(jnp.logical_or(k != r, off))(lambda k=k: gp_copy(k).start())
    gq0[c] = gains[...]

    @pl.when(diag)
    def _():
        gp0[c] = gains[...]

    rows_step = 32
    lane = lax.broadcasted_iota(jnp.int32, (rows_step, block), 1) + c * block
    sub = lax.broadcasted_iota(jnp.int32, (rows_step, block), 0) + r * block

    @pl.loop(0, block // rows_step)
    def _(s):
        rows = pl.ds(pl.multiple_of(s * rows_step, rows_step), rows_step)
        pair = sky[rows].astype(jnp.float32)
        mr, mi = pair[:, 0, :], pair[:, 1, :]
        keep = sub + s * rows_step != lane
        mr = jnp.where(keep, mr, 0.0)
        mi = jnp.where(keep, mi, 0.0)
        model[0, rows, :] = mr
        model[1, rows, :] = mi
        power[rows, :] = mr * mr + mi * mi
        vr[rows, :] = jnp.zeros((rows_step, block), jnp.float32)
        vi[rows, :] = jnp.zeros((rows_step, block), jnp.float32)

    mine = pltpu.make_async_copy(mine_at(jnp.where(r < c, 0, 1)), right.at[r], local_sem.at[1])
    mine.start()
    mine.wait()

    def multiply(a_ref, b_ref, k, s):
        rows = pl.ds(pl.multiple_of(s * tile, tile), tile)
        ar, ai = a_ref[k, 0, rows, :], a_ref[k, 1, rows, :]
        br, bi = b_ref[k, 0], b_ref[k, 1]
        dot = functools.partial(
            lax.dot_general, dimension_numbers=CONTRACT_LAST, preferred_element_type=jnp.float32
        )
        both = lambda x, y: jnp.concatenate([x, y], axis=1)
        vr[rows, :] += dot(both(ar, ai), both(br, bi))
        vi[rows, :] += dot(both(ai, -ar), both(br, bi))

    @pl.when(diag)
    def _():
        copy = pltpu.make_async_copy(mine_at(0), left.at[r], local_sem.at[0])
        copy.start()
        copy.wait()

        @pl.loop(0, len(chunks))
        def _(s):
            multiply(left, left, r, s)
            multiply(right, right, r, s)

    def onward_copy(k, s, onward):
        return remote(
            part_of(chain, k, s), part_of(chain, k, s), fwd_send.at[k, s], chain_recv.at[k, s], r, c + onward
        )

    def arrived(k, s, onward):
        landed(part_of(chain, k, s), chain_recv.at[k, s])
        pl.when(jnp.logical_and(c + onward >= 0, c + onward < n))(lambda: onward_copy(k, s, onward).start())
        pl.when(k != r)(lambda: left_copy(k, s).start())

    for s in chunks:
        for step in range(1, n):
            pl.when(c >= step)(lambda: arrived(c - step, s, 1))
            pl.when(c + step < n)(lambda: arrived(c + step, s, -1))
            if step == 1 and s + ahead < len(chunks):
                inner = jnp.logical_and(c > 0, c < n - 1)
                pl.when(inner)(lambda: up(s + ahead).start())
                pl.when(inner)(lambda: down(s + ahead).start())

    @pl.when(off)
    def _():
        @pl.loop(0, len(chunks))
        def _(s):
            multiply(chain, right, r, s)

    for k in range(n):
        pl.when(k != c)(lambda k=k: landed(gq0.at[k], gq_recv.at[k]))
        pl.when(jnp.logical_or(k != c, off))(lambda k=k: landed(gp0.at[k], gp_recv.at[k]))

    def start_gains(ref):
        return [jnp.concatenate([ref[k, part : part + 1, :] for k in range(n)], axis=1) for part in range(2)]

    gp = start_gains(gp0)
    gq = start_gains(gq0)
    lanes = 128

    def lay_out(gains_row):
        qr[...] = jnp.broadcast_to(gains_row[0], (lanes, block)).T
        qi[...] = jnp.broadcast_to(gains_row[1], (lanes, block)).T

    lay_out(gq)

    for step in range(1, n):
        landed(right.at[lax.rem(r + step, n)], right_recv.at[lax.rem(r + step, n)])

    @pl.loop(0, len(chunks))
    def _(s):
        @pl.loop(1, n)
        def _(step):
            k = lax.rem(r + step, n)
            rows = pl.ds(pl.multiple_of(s * tile, tile), tile)
            landed(left.at[k, :, rows, :], left_recv.at[k, s])
            pl.when(off)(lambda: multiply(left, right, k, s))

    @pl.when(diag)
    def _():
        @pl.loop(1, n)
        def _(step):
            k = lax.rem(r + step, n)

            @pl.loop(0, len(chunks))
            def _(s):
                multiply(left, left, k, s)
                multiply(right, right, k, s)

    @pl.loop(0, block // rows_step)
    def _(s):
        rows = pl.ds(pl.multiple_of(s * rows_step, rows_step), rows_step)
        mr, mi = model[0, rows, :], model[1, rows, :]
        a, b = vr[rows, :], vi[rows, :]
        vr[rows, :] = a * mr + b * mi
        vi[rows, :] = a * mi - b * mr

    for it in range(ITERS):
        if it > 0:
            lay_out(gq)
        width = max(block // 2, lanes)
        for start in range(0, block, width):
            columns = pl.ds(start, width)
            gpr = jnp.broadcast_to(gp[0][:, start : start + width], (8, width))
            gpi = jnp.broadcast_to(gp[1][:, start : start + width], (8, width))

            def fold(x):
                total = x[:, :lanes]
                for t in range(lanes, width, lanes):
                    total = total + x[:, t : t + lanes]
                return total

            def sums(s, carry):
                sum_r, sum_i, sum_e = carry
                rows = pl.ds(pl.multiple_of(s * 8, 8), 8)
                wr, wi = vr[rows, columns], vi[rows, columns]
                ar, ai = qr[rows, :], qi[rows, :]
                norm = ar * ar + ai * ai
                wide = lambda x: jnp.concatenate([x] * (width // lanes), axis=1)
                ar, ai, norm = wide(ar), wide(ai), wide(norm)
                row_r = fold(wr * gpr + wi * gpi)
                row_i = fold(wr * gpi - wi * gpr)
                if start > 0:
                    row_r = row_r + tr[rows, :]
                    row_i = row_i + ti[rows, :]
                tr[rows, :] = row_r
                ti[rows, :] = row_i
                return (
                    sum_r + (wr * ar - wi * ai),
                    sum_i + (wr * ai + wi * ar),
                    sum_e + power[rows, columns] * norm,
                )

            zero = jnp.zeros((8, width), jnp.float32)
            found = lax.fori_loop(0, block // 8, sums, (zero, zero, zero), unroll=4)
            for part, value in enumerate(found):
                abuf[it, part : part + 1, columns] = jnp.sum(value, axis=0, keepdims=True)
        for part, ref in enumerate((tr, ti)):
            bbuf[it, part : part + 1, :] = jnp.sum(ref[...].T, axis=0, keepdims=True)

        a_copy = remote(abuf.at[it], ain.at[it, r], a_send.at[it], a_recv.at[it, r], c, c)
        b_copy = remote(bbuf.at[it], bin_.at[it, c], b_send.at[it], b_recv.at[it, c], r, r)

        @pl.when(off)
        def _():
            a_copy.start()
            b_copy.start()

        def p_copy(i):
            return remote(gin.at[it, 0], gin.at[it, 0], g_send.at[it, 0, i], g_recv.at[it, 0], i, c)

        def q_copy(j):
            return remote(gin.at[it, 0], gin.at[it, 1], g_send.at[it, 1, j], g_recv.at[it, 1], r, j)

        @pl.when(diag)
        def _():
            total = abuf[it]
            for k in range(n):
                @pl.when(k != r)
                def _():
                    landed(ain.at[it, k], a_recv.at[it, k])
                    landed(bin_.at[it, k], b_recv.at[it, k])

            ain[it, r] = jnp.zeros_like(total)
            bin_[it, r] = jnp.zeros((2, block), jnp.float32)
            for k in range(n):
                total = total + ain[it, k]
            extra = bin_[it, 0]
            for k in range(1, n):
                extra = extra + bin_[it, k]
            for part in range(2):
                fresh = (total[part : part + 1] + extra[part : part + 1]) / total[2:3]
                if it == 1:
                    fresh = 0.5 * (fresh + gin[0, 0, part : part + 1, :])
                gin[it, 0, part : part + 1, :] = fresh
                gin[it, 1, part : part + 1, :] = fresh
            for k in range(n):
                @pl.when(k != r)
                def _():
                    q_copy(k).start()
                    if it < ITERS - 1:
                        p_copy(k).start()

        @pl.when(off)
        def _():
            landed(gin.at[it, 1], g_recv.at[it, 1])
            if it < ITERS - 1:
                landed(gin.at[it, 0], g_recv.at[it, 0])

        gp = [gin[it, 0, part : part + 1, :] for part in range(2)]
        gq = [gin[it, 1, part : part + 1, :] for part in range(2)]

    out[...] = gin[ITERS - 1, 1, 0:2, pl.ds(pl.multiple_of(c * share, share), share)]

    for step in range(1, n):
        right_copy(lax.rem(r + step, n)).wait_send()

    def gone(k, s, onward):
        pl.when(jnp.logical_and(c + onward >= 0, c + onward < n))(lambda: onward_copy(k, s, onward).wait_send())
        pl.when(k != r)(lambda: left_copy(k, s).wait_send())

    for s in chunks:
        pl.when(c < n - 1)(lambda: up(s).wait_send())
        pl.when(c > 0)(lambda: down(s).wait_send())
        pl.when(off)(lambda: own_left_copy(s).wait_send())
        for step in range(1, n):
            pl.when(c >= step)(lambda: gone(c - step, s, 1))
            pl.when(c + step < n)(lambda: gone(c + step, s, -1))
    for k in range(n):
        pl.when(k != c)(lambda k=k: gq_copy(k).wait_send())
        pl.when(jnp.logical_or(k != r, off))(lambda k=k: gp_copy(k).wait_send())
    for it in range(ITERS):
        a_copy = remote(abuf.at[it], ain.at[it, r], a_send.at[it], a_recv.at[it, r], c, c)
        b_copy = remote(bbuf.at[it], bin_.at[it, c], b_send.at[it], b_recv.at[it, c], r, r)

        @pl.when(off)
        def _():
            a_copy.wait_send()
            b_copy.wait_send()

        for k in range(n):
            @pl.when(jnp.logical_and(diag, k != r))
            def _():
                remote(gin.at[it, 0], gin.at[it, 1], g_send.at[it, 1, k], g_recv.at[it, 1], r, k).wait_send()
                if it < ITERS - 1:
                    remote(gin.at[it, 0], gin.at[it, 0], g_send.at[it, 0, k], g_recv.at[it, 0], k, c).wait_send()


def square_body(n, samples, sky_model, initial_gains):
    block, _, times = samples.shape
    half = times // 2
    parts = samples.transpose(1, 0, 2)
    share = initial_gains.shape[1]
    dma = pltpu.SemaphoreType.DMA
    vmem = pltpu.VMEM
    f32, bf16 = jnp.float32, jnp.bfloat16
    piece = (n, 2, block, half)
    return pl.pallas_call(
        functools.partial(calibrate, n),
        out_shape=jax.ShapeDtypeStruct((2, share), f32),
        in_specs=[pl.BlockSpec(memory_space=pltpu.VMEM)] * 3,
        out_specs=pl.BlockSpec(memory_space=pltpu.VMEM),
        scratch_shapes=[
            vmem(piece, bf16),
            vmem(piece, bf16),
            vmem(piece, bf16),
            vmem((block, block), f32),
            vmem((block, block), f32),
            vmem((block, block), f32),
            vmem((2, block, block), f32),
            vmem((block, 128), f32),
            vmem((block, 128), f32),
            vmem((block, 128), f32),
            vmem((block, 128), f32),
            vmem((n, 2, share), f32),
            vmem((n, 2, share), f32),
            vmem((ITERS, 4, block), f32),
            vmem((ITERS, 2, block), f32),
            vmem((ITERS, n, 4, block), f32),
            vmem((ITERS, n, 2, block), f32),
            vmem((ITERS, 2, 2, block), f32),
            dma((2, CHUNKS)), dma((n, CHUNKS)), dma((n, CHUNKS)),
            dma((n, CHUNKS)), dma((n, CHUNKS)), dma((n,)), dma((n,)), dma((2,)),
            dma((n,)), dma((n,)), dma((n,)), dma((n,)),
            dma((ITERS,)), dma((ITERS, n)), dma((ITERS,)), dma((ITERS, n)),
            dma((ITERS, 2, n)), dma((ITERS, 2)),
        ],
        compiler_params=pltpu.CompilerParams(
            collective_id=0, has_side_effects=True, vmem_limit_bytes=56 * 1024 * 1024
        ),
        cost_estimate=pl.CostEstimate(
            flops=8 * block * block * times * n // 2, bytes_accessed=8 * block * block, transcendentals=0
        ),
    )(parts, sky_model, initial_gains)


def body(samples, sky_model, initial_gains):
    row_count = lax.axis_size("row")
    column_count = lax.axis_size("col")
    row_index = lax.axis_index("row")
    column_index = lax.axis_index("col")
    block_column = samples.shape[0]
    block_row = sky_model.shape[0]
    share_size = initial_gains.shape[1]
    contract_last = (((1,), (1,)), ((), ()))
    upper_limit = lax.Precision.HIGHEST
    own_start = (row_index * column_count + column_index) * share_size
    flattened = samples.reshape(block_column, -1)
    rotated = jnp.concatenate([-samples[:, 1, :], samples[:, 0, :]], axis=1)
    right_side = jnp.concatenate([flattened, rotated], axis=0)
    all_antennas = lax.all_gather(flattened, "col", axis=0, tiled=True)
    vis_tile = lax.psum_scatter(
        lax.dot_general(
            all_antennas, right_side, contract_last, preferred_element_type=jnp.float32
        ),
        "row",
        scatter_dimension=0,
        tiled=True,
    )
    vis_real = vis_tile[:, :block_column]
    vis_imag = vis_tile[:, block_column:]
    model_real = sky_model[:, 0, :].astype(jnp.float32)
    model_imag = sky_model[:, 1, :].astype(jnp.float32)
    global_rows = row_index * block_row + lax.broadcasted_iota(
        jnp.int32, (block_row, block_column), 0
    )
    global_columns = column_index * block_column + lax.broadcasted_iota(
        jnp.int32, (block_row, block_column), 1
    )
    cross_mask = (global_rows != global_columns).astype(jnp.float32)
    weight_real = (vis_real * model_real + vis_imag * model_imag) * cross_mask
    weight_imag = (vis_real * model_imag - vis_imag * model_real) * cross_mask
    model_power = (model_real * model_real + model_imag * model_imag) * cross_mask
    stacked = jnp.concatenate([weight_real, weight_imag], axis=0)
    row_gains = lax.all_gather(initial_gains, "col", axis=1, tiled=True)
    everything = row_gains
    for iteration in range(ITERS):
        gain_real = row_gains[0]
        gain_imag = row_gains[1]
        left_rows = jnp.stack(
            [jnp.concatenate([gain_real, -gain_imag]), jnp.concatenate([gain_imag, gain_real])]
        )
        totals = jnp.dot(left_rows, stacked, precision=upper_limit)
        energy = jnp.dot(
            gain_real * gain_real + gain_imag * gain_imag, model_power, precision=upper_limit
        )
        totals, energy = (totals, energy)
        totals, energy = (
            lax.psum_scatter(totals, "row", scatter_dimension=1, tiled=True),
            lax.psum_scatter(energy, "row", scatter_dimension=0, tiled=True),
        )
        updated = totals / energy[None, :]
        if iteration == 1:
            previous = lax.dynamic_slice_in_dim(
                everything, (column_index * row_count + row_index) * share_size, share_size, 1
            )
            updated = 0.5 * (updated + previous)
        gain_block = lax.all_gather(updated, "row", axis=1, tiled=True)
        everything = lax.all_gather(gain_block, "col", axis=1, tiled=True)
        row_gains = lax.dynamic_slice_in_dim(everything, row_index * block_row, block_row, 1)
    return lax.dynamic_slice_in_dim(everything, own_start, share_size, 1)


def solution(mesh):
    n = mesh.shape["row"]
    square = n == mesh.shape["col"]
    return jax.shard_map(
        functools.partial(square_body, n) if square else body,
        mesh=mesh,
        in_specs=(
            P(("chan", "col"), None, "row"),
            P(("chan", "row"), None, "col"),
            P(None, ("chan", "row", "col")),
        ),
        out_specs=P(None, ("chan", "row", "col")),
        check_vma=False,
    )
```

```python
import functools

import jax
import jax.numpy as jnp
from jax import lax
from jax.experimental import pallas as pl
from jax.experimental.pallas import tpu as pltpu
from jax.sharding import PartitionSpec as P

ITERS = 3
CHUNKS = 4
MESH = pl.DeviceIdType.MESH
CONTRACT_LAST = (((1,), (1,)), ((), ()))


def remote(src, dst, send, recv, row, col):
    return pltpu.make_async_remote_copy(
        src_ref=src,
        dst_ref=dst,
        send_sem=send,
        recv_sem=recv,
        device_id={"row": row, "col": col},
        device_id_type=MESH,
    )


def landed(ref, sem):
    pltpu.make_async_copy(ref, ref, sem).wait()


def calibrate(
    n, own, sky_model, gains, out, sky, chain, left, right, vr, vi, power, model, qr, qi, tr, ti, gp0, gq0,
    abuf, bbuf, ain, bin_, gin,
    up_send, fwd_send, chain_recv, left_send, left_recv, right_send, right_recv, local_sem,
    gp_send, gp_recv, gq_send, gq_recv, a_send, a_recv, b_send, b_recv, g_send, g_recv,
):
    r = lax.axis_index("row")
    c = lax.axis_index("col")
    block = own.shape[1]
    half = own.shape[2] // 2
    share = gains.shape[1]

    tile = max(block // CHUNKS, 16)
    chunks = range(block // tile)

    def mine_at(h):
        return own.at[:, :, pl.ds(pl.multiple_of(h * half, half), half)]

    def part_of(ref, k, s):
        return ref.at[k, :, pl.ds(s * tile, tile), :]

    def mine_part(h, s):
        return own.at[:, pl.ds(s * tile, tile), pl.ds(h * half, half)]

    diag = r == c
    off = r != c

    sky_copy = pltpu.make_async_copy(sky_model, sky, local_sem.at[0])
    sky_copy.start()

    barrier = pltpu.get_barrier_semaphore()
    for step in range(1, n * n):
        other = lax.rem(r * n + c + step, n * n)
        pl.semaphore_signal(
            barrier, inc=1, device_id={"row": other // n, "col": lax.rem(other, n)}, device_id_type=MESH
        )
    pl.semaphore_wait(barrier, n * n - 1)

    def up(s):
        return remote(mine_part(0, s), part_of(chain, c, s), up_send.at[0, s], chain_recv.at[c, s], r, c + 1)

    def down(s):
        return remote(mine_part(1, s), part_of(chain, c, s), up_send.at[1, s], chain_recv.at[c, s], r, c - 1)

    ahead = 2
    for s in chunks:
        first = s < ahead
        pl.when(c < n - 1 if first else c == 0)(lambda: up(s).start())
        pl.when(c > 0 if first else c == n - 1)(lambda: down(s).start())

    def right_copy(k):
        h = jnp.where(k < c, 0, 1)
        return remote(mine_at(h), right.at[r], right_send.at[k], right_recv.at[r], k, c)

    def left_copy(k, s):
        return remote(
            part_of(chain, k, s), part_of(left, r, s), left_send.at[k, s], left_recv.at[r, s], k, c
        )

    def own_left_copy(s):
        return remote(
            mine_part(0, s), part_of(left, r, s), left_send.at[c, s], left_recv.at[r, s], c, c
        )

    for step in range(1, n):
        right_copy(lax.rem(r + step, n)).start()
    for s in chunks:
        pl.when(off)(lambda: own_left_copy(s).start())

    def gq_copy(j):
        return remote(gains, gq0.at[c], gq_send.at[j], gq_recv.at[c], r, j)

    def gp_copy(i):
        return remote(gains, gp0.at[c], gp_send.at[i], gp_recv.at[c], i, r)

    for k in range(n):
        pl.when(k != c)(lambda k=k: gq_copy(k).start())
        pl.when(jnp.logical_or(k != r, off))(lambda k=k: gp_copy(k).start())
    gq0[c] = gains[...]

    @pl.when(diag)
    def _():
        gp0[c] = gains[...]

    sky_copy.wait()

    rows_step = 32
    lane = lax.broadcasted_iota(jnp.int32, (rows_step, block), 1) + c * block
    sub = lax.broadcasted_iota(jnp.int32, (rows_step, block), 0) + r * block

    @pl.loop(0, block // rows_step)
    def _(s):
        rows = pl.ds(pl.multiple_of(s * rows_step, rows_step), rows_step)
        pair = sky[rows].astype(jnp.float32)
        mr, mi = pair[:, 0, :], pair[:, 1, :]
        keep = sub + s * rows_step != lane
        mr = jnp.where(keep, mr, 0.0)
        mi = jnp.where(keep, mi, 0.0)
        model[0, rows, :] = mr
        model[1, rows, :] = mi
        power[rows, :] = mr * mr + mi * mi
        vr[rows, :] = jnp.zeros((rows_step, block), jnp.float32)
        vi[rows, :] = jnp.zeros((rows_step, block), jnp.float32)

    mine = pltpu.make_async_copy(mine_at(jnp.where(r < c, 0, 1)), right.at[r], local_sem.at[1])
    mine.start()
    mine.wait()

    def multiply(a_ref, b_ref, k, s):
        rows = pl.ds(pl.multiple_of(s * tile, tile), tile)
        ar, ai = a_ref[k, 0, rows, :], a_ref[k, 1, rows, :]
        br, bi = b_ref[k, 0], b_ref[k, 1]
        dot = functools.partial(
            lax.dot_general, dimension_numbers=CONTRACT_LAST, preferred_element_type=jnp.float32
        )
        both = lambda x, y: jnp.concatenate([x, y], axis=1)
        found = dot(jnp.concatenate([both(ar, ai), both(ai, -ar)], axis=0), both(br, bi))
        vr[rows, :] += found[:tile]
        vi[rows, :] += found[tile:]

    def square(ref, k):
        @pl.loop(0, len(chunks))
        def _(s):
            multiply(ref, ref, k, s)

    @pl.when(diag)
    def _():
        copy = pltpu.make_async_copy(mine_at(0), left.at[r], local_sem.at[0])
        copy.start()
        copy.wait()

        square(left, r)
        square(right, r)

    def onward_copy(k, s, onward):
        return remote(
            part_of(chain, k, s), part_of(chain, k, s), fwd_send.at[k, s], chain_recv.at[k, s], r, c + onward
        )

    def arrived(k, s, onward):
        landed(part_of(chain, k, s), chain_recv.at[k, s])
        pl.when(jnp.logical_and(c + onward >= 0, c + onward < n))(lambda: onward_copy(k, s, onward).start())
        pl.when(k != r)(lambda: left_copy(k, s).start())

    for s in chunks:
        for step in range(1, n):
            pl.when(c >= step)(lambda: arrived(c - step, s, 1))
            pl.when(c + step < n)(lambda: arrived(c + step, s, -1))
            if step == 1 and s + ahead < len(chunks):
                inner = jnp.logical_and(c > 0, c < n - 1)
                pl.when(inner)(lambda: up(s + ahead).start())
                pl.when(inner)(lambda: down(s + ahead).start())

    @pl.when(off)
    def _():
        @pl.loop(0, len(chunks))
        def _(s):
            multiply(chain, right, r, s)

    for k in range(n):
        pl.when(k != c)(lambda k=k: landed(gq0.at[k], gq_recv.at[k]))
        pl.when(jnp.logical_or(k != c, off))(lambda k=k: landed(gp0.at[k], gp_recv.at[k]))

    def start_gains(ref):
        return [jnp.concatenate([ref[k, part : part + 1, :] for k in range(n)], axis=1) for part in range(2)]

    gp = start_gains(gp0)
    gq = start_gains(gq0)
    lanes = 128

    def lay_out(gains_row):
        qr[...] = jnp.broadcast_to(gains_row[0], (lanes, block)).T
        qi[...] = jnp.broadcast_to(gains_row[1], (lanes, block)).T

    lay_out(gq)

    @pl.when(off)
    def _():
        for step in range(1, n):
            k = lax.rem(r + step, n)
            landed(right.at[k], right_recv.at[k])

        @pl.loop(0, len(chunks))
        def _(s):
            @pl.loop(1, n)
            def _(step):
                k = lax.rem(r + step, n)
                rows = pl.ds(pl.multiple_of(s * tile, tile), tile)
                landed(left.at[k, :, rows, :], left_recv.at[k, s])
                multiply(left, right, k, s)

    @pl.when(diag)
    def _():
        @pl.loop(1, n)
        def _(step):
            k = lax.rem(r + step, n)
            landed(right.at[k], right_recv.at[k])
            square(right, k)

        @pl.loop(1, n)
        def _(step):
            k = lax.rem(r + step, n)
            for s in chunks:
                landed(part_of(left, k, s), left_recv.at[k, s])
            square(left, k)

    @pl.loop(0, block // rows_step)
    def _(s):
        rows = pl.ds(pl.multiple_of(s * rows_step, rows_step), rows_step)
        mr, mi = model[0, rows, :], model[1, rows, :]
        a, b = vr[rows, :], vi[rows, :]
        vr[rows, :] = a * mr + b * mi
        vi[rows, :] = a * mi - b * mr

    for it in range(ITERS):
        if it > 0:
            lay_out(gq)
        width = max(block // 2, lanes)
        for start in range(0, block, width):
            columns = pl.ds(start, width)
            gpr = jnp.broadcast_to(gp[0][:, start : start + width], (8, width))
            gpi = jnp.broadcast_to(gp[1][:, start : start + width], (8, width))

            def fold(x):
                total = x[:, :lanes]
                for t in range(lanes, width, lanes):
                    total = total + x[:, t : t + lanes]
                return total

            def sums(s, carry):
                sum_r, sum_i, sum_e = carry
                rows = pl.ds(pl.multiple_of(s * 8, 8), 8)
                wr, wi = vr[rows, columns], vi[rows, columns]
                ar, ai = qr[rows, :], qi[rows, :]
                norm = ar * ar + ai * ai
                wide = lambda x: jnp.concatenate([x] * (width // lanes), axis=1)
                ar, ai, norm = wide(ar), wide(ai), wide(norm)
                row_r = fold(wr * gpr + wi * gpi)
                row_i = fold(wr * gpi - wi * gpr)
                if start > 0:
                    row_r = row_r + tr[rows, :]
                    row_i = row_i + ti[rows, :]
                tr[rows, :] = row_r
                ti[rows, :] = row_i
                return (
                    sum_r + (wr * ar - wi * ai),
                    sum_i + (wr * ai + wi * ar),
                    sum_e + power[rows, columns] * norm,
                )

            zero = jnp.zeros((8, width), jnp.float32)
            found = lax.fori_loop(0, block // 8, sums, (zero, zero, zero), unroll=4)
            for part, value in enumerate(found):
                abuf[it, part : part + 1, columns] = jnp.sum(value, axis=0, keepdims=True)
        for part, ref in enumerate((tr, ti)):
            bbuf[it, part : part + 1, :] = jnp.sum(ref[...].T, axis=0, keepdims=True)

        a_copy = remote(abuf.at[it], ain.at[it, r], a_send.at[it], a_recv.at[it, r], c, c)
        b_copy = remote(bbuf.at[it], bin_.at[it, c], b_send.at[it], b_recv.at[it, c], r, r)

        @pl.when(off)
        def _():
            a_copy.start()
            b_copy.start()

        def p_copy(i):
            return remote(gin.at[it, 0], gin.at[it, 0], g_send.at[it, 0, i], g_recv.at[it, 0], i, c)

        def q_copy(j):
            return remote(gin.at[it, 0], gin.at[it, 1], g_send.at[it, 1, j], g_recv.at[it, 1], r, j)

        @pl.when(diag)
        def _():
            total = abuf[it]
            for k in range(n):
                @pl.when(k != r)
                def _():
                    landed(ain.at[it, k], a_recv.at[it, k])
                    landed(bin_.at[it, k], b_recv.at[it, k])

            ain[it, r] = jnp.zeros_like(total)
            bin_[it, r] = jnp.zeros((2, block), jnp.float32)
            for k in range(n):
                total = total + ain[it, k]
            extra = bin_[it, 0]
            for k in range(1, n):
                extra = extra + bin_[it, k]
            for part in range(2):
                fresh = (total[part : part + 1] + extra[part : part + 1]) / total[2:3]
                if it == 1:
                    fresh = 0.5 * (fresh + gin[0, 0, part : part + 1, :])
                gin[it, 0, part : part + 1, :] = fresh
                gin[it, 1, part : part + 1, :] = fresh
            for k in range(n):
                @pl.when(k != r)
                def _():
                    q_copy(k).start()
                    if it < ITERS - 1:
                        p_copy(k).start()

        @pl.when(off)
        def _():
            landed(gin.at[it, 1], g_recv.at[it, 1])
            if it < ITERS - 1:
                landed(gin.at[it, 0], g_recv.at[it, 0])

        gp = [gin[it, 0, part : part + 1, :] for part in range(2)]
        gq = [gin[it, 1, part : part + 1, :] for part in range(2)]

    out[...] = gin[ITERS - 1, 1, 0:2, pl.ds(pl.multiple_of(c * share, share), share)]

    for step in range(1, n):
        right_copy(lax.rem(r + step, n)).wait_send()

    def gone(k, s, onward):
        pl.when(jnp.logical_and(c + onward >= 0, c + onward < n))(lambda: onward_copy(k, s, onward).wait_send())
        pl.when(k != r)(lambda: left_copy(k, s).wait_send())

    for s in chunks:
        pl.when(c < n - 1)(lambda: up(s).wait_send())
        pl.when(c > 0)(lambda: down(s).wait_send())
        pl.when(off)(lambda: own_left_copy(s).wait_send())
        for step in range(1, n):
            pl.when(c >= step)(lambda: gone(c - step, s, 1))
            pl.when(c + step < n)(lambda: gone(c + step, s, -1))
    for k in range(n):
        pl.when(k != c)(lambda k=k: gq_copy(k).wait_send())
        pl.when(jnp.logical_or(k != r, off))(lambda k=k: gp_copy(k).wait_send())
    for it in range(ITERS):
        a_copy = remote(abuf.at[it], ain.at[it, r], a_send.at[it], a_recv.at[it, r], c, c)
        b_copy = remote(bbuf.at[it], bin_.at[it, c], b_send.at[it], b_recv.at[it, c], r, r)

        @pl.when(off)
        def _():
            a_copy.wait_send()
            b_copy.wait_send()

        for k in range(n):
            @pl.when(jnp.logical_and(diag, k != r))
            def _():
                remote(gin.at[it, 0], gin.at[it, 1], g_send.at[it, 1, k], g_recv.at[it, 1], r, k).wait_send()
                if it < ITERS - 1:
                    remote(gin.at[it, 0], gin.at[it, 0], g_send.at[it, 0, k], g_recv.at[it, 0], k, c).wait_send()


def square_body(n, samples, sky_model, initial_gains):
    block, _, times = samples.shape
    half = times // 2
    parts = samples.transpose(1, 0, 2)
    share = initial_gains.shape[1]
    dma = pltpu.SemaphoreType.DMA
    vmem = pltpu.VMEM
    f32, bf16 = jnp.float32, jnp.bfloat16
    piece = (n, 2, block, half)
    return pl.pallas_call(
        functools.partial(calibrate, n),
        out_shape=jax.ShapeDtypeStruct((2, share), f32),
        in_specs=[
            pl.BlockSpec(memory_space=pltpu.VMEM),
            pl.BlockSpec(memory_space=pl.ANY),
            pl.BlockSpec(memory_space=pltpu.VMEM),
        ],
        out_specs=pl.BlockSpec(memory_space=pltpu.VMEM),
        scratch_shapes=[
            vmem(sky_model.shape, bf16),
            vmem(piece, bf16),
            vmem(piece, bf16),
            vmem(piece, bf16),
            vmem((block, block), f32),
            vmem((block, block), f32),
            vmem((block, block), f32),
            vmem((2, block, block), f32),
            vmem((block, 128), f32),
            vmem((block, 128), f32),
            vmem((block, 128), f32),
            vmem((block, 128), f32),
            vmem((n, 2, share), f32),
            vmem((n, 2, share), f32),
            vmem((ITERS, 4, block), f32),
            vmem((ITERS, 2, block), f32),
            vmem((ITERS, n, 4, block), f32),
            vmem((ITERS, n, 2, block), f32),
            vmem((ITERS, 2, 2, block), f32),
            dma((2, CHUNKS)), dma((n, CHUNKS)), dma((n, CHUNKS)),
            dma((n, CHUNKS)), dma((n, CHUNKS)), dma((n,)), dma((n,)), dma((2,)),
            dma((n,)), dma((n,)), dma((n,)), dma((n,)),
            dma((ITERS,)), dma((ITERS, n)), dma((ITERS,)), dma((ITERS, n)),
            dma((ITERS, 2, n)), dma((ITERS, 2)),
        ],
        compiler_params=pltpu.CompilerParams(
            collective_id=0, has_side_effects=True, vmem_limit_bytes=56 * 1024 * 1024
        ),
        cost_estimate=pl.CostEstimate(
            flops=8 * block * block * times * n // 2, bytes_accessed=8 * block * block, transcendentals=0
        ),
    )(parts, sky_model, initial_gains)


def body(samples, sky_model, initial_gains):
    row_count = lax.axis_size("row")
    column_count = lax.axis_size("col")
    row_index = lax.axis_index("row")
    column_index = lax.axis_index("col")
    block_column = samples.shape[0]
    block_row = sky_model.shape[0]
    share_size = initial_gains.shape[1]
    contract_last = (((1,), (1,)), ((), ()))
    upper_limit = lax.Precision.HIGHEST
    own_start = (row_index * column_count + column_index) * share_size
    flattened = samples.reshape(block_column, -1)
    rotated = jnp.concatenate([-samples[:, 1, :], samples[:, 0, :]], axis=1)
    right_side = jnp.concatenate([flattened, rotated], axis=0)
    all_antennas = lax.all_gather(flattened, "col", axis=0, tiled=True)
    vis_tile = lax.psum_scatter(
        lax.dot_general(
            all_antennas, right_side, contract_last, preferred_element_type=jnp.float32
        ),
        "row",
        scatter_dimension=0,
        tiled=True,
    )
    vis_real = vis_tile[:, :block_column]
    vis_imag = vis_tile[:, block_column:]
    model_real = sky_model[:, 0, :].astype(jnp.float32)
    model_imag = sky_model[:, 1, :].astype(jnp.float32)
    global_rows = row_index * block_row + lax.broadcasted_iota(
        jnp.int32, (block_row, block_column), 0
    )
    global_columns = column_index * block_column + lax.broadcasted_iota(
        jnp.int32, (block_row, block_column), 1
    )
    cross_mask = (global_rows != global_columns).astype(jnp.float32)
    weight_real = (vis_real * model_real + vis_imag * model_imag) * cross_mask
    weight_imag = (vis_real * model_imag - vis_imag * model_real) * cross_mask
    model_power = (model_real * model_real + model_imag * model_imag) * cross_mask
    stacked = jnp.concatenate([weight_real, weight_imag], axis=0)
    row_gains = lax.all_gather(initial_gains, "col", axis=1, tiled=True)
    everything = row_gains
    for iteration in range(ITERS):
        gain_real = row_gains[0]
        gain_imag = row_gains[1]
        left_rows = jnp.stack(
            [jnp.concatenate([gain_real, -gain_imag]), jnp.concatenate([gain_imag, gain_real])]
        )
        totals = jnp.dot(left_rows, stacked, precision=upper_limit)
        energy = jnp.dot(
            gain_real * gain_real + gain_imag * gain_imag, model_power, precision=upper_limit
        )
        totals, energy = (totals, energy)
        totals, energy = (
            lax.psum_scatter(totals, "row", scatter_dimension=1, tiled=True),
            lax.psum_scatter(energy, "row", scatter_dimension=0, tiled=True),
        )
        updated = totals / energy[None, :]
        if iteration == 1:
            previous = lax.dynamic_slice_in_dim(
                everything, (column_index * row_count + row_index) * share_size, share_size, 1
            )
            updated = 0.5 * (updated + previous)
        gain_block = lax.all_gather(updated, "row", axis=1, tiled=True)
        everything = lax.all_gather(gain_block, "col", axis=1, tiled=True)
        row_gains = lax.dynamic_slice_in_dim(everything, row_index * block_row, block_row, 1)
    return lax.dynamic_slice_in_dim(everything, own_start, share_size, 1)


def solution(mesh):
    n = mesh.shape["row"]
    square = n == mesh.shape["col"]
    return jax.shard_map(
        functools.partial(square_body, n) if square else body,
        mesh=mesh,
        in_specs=(
            P(("chan", "col"), None, "row"),
            P(("chan", "row"), None, "col"),
            P(None, ("chan", "row", "col")),
        ),
        out_specs=P(None, ("chan", "row", "col")),
        check_vma=False,
    )
```

```python
import functools

import jax
import jax.numpy as jnp
from jax import lax
from jax.experimental import pallas as pl
from jax.experimental.pallas import tpu as pltpu
from jax.sharding import PartitionSpec as P

ITERS = 3
CHUNKS = 4
MESH = pl.DeviceIdType.MESH
CONTRACT_LAST = (((1,), (1,)), ((), ()))


def remote(src, dst, send, recv, row, col):
    return pltpu.make_async_remote_copy(
        src_ref=src,
        dst_ref=dst,
        send_sem=send,
        recv_sem=recv,
        device_id={"row": row, "col": col},
        device_id_type=MESH,
    )


def landed(ref, sem):
    pltpu.make_async_copy(ref, ref, sem).wait()


def calibrate(
    n, samples, sky_model, gains, out, own, sky, chain, left, right, vr, vi, power, model, qr, qi, tr, ti, gp0, gq0,
    abuf, bbuf, ain, bin_, gin,
    up_send, fwd_send, chain_recv, left_send, left_recv, right_send, right_recv, local_sem,
    gp_send, gp_recv, gq_send, gq_recv, a_send, a_recv, b_send, b_recv, g_send, g_recv,
):
    r = lax.axis_index("row")
    c = lax.axis_index("col")
    block = own.shape[1]
    half = own.shape[2] // 2
    share = gains.shape[1]

    tile = max(block // CHUNKS, 16)
    chunks = range(block // tile)

    def mine_at(h):
        return own.at[:, :, pl.ds(pl.multiple_of(h * half, half), half)]

    def part_of(ref, k, s):
        return ref.at[k, :, pl.ds(s * tile, tile), :]

    def mine_part(h, s):
        return own.at[:, pl.ds(s * tile, tile), pl.ds(h * half, half)]

    diag = r == c
    off = r != c

    sky_copy = pltpu.make_async_copy(sky_model, sky, local_sem.at[0])
    sky_copy.start()

    barrier = pltpu.get_barrier_semaphore()
    for step in range(1, n * n):
        other = lax.rem(r * n + c + step, n * n)
        pl.semaphore_signal(
            barrier, inc=1, device_id={"row": other // n, "col": lax.rem(other, n)}, device_id_type=MESH
        )

    @pl.loop(0, block // 32)
    def _(s):
        rows = pl.ds(pl.multiple_of(s * 32, 32), 32)
        pair = samples[rows].astype(jnp.float32)
        own[0, rows, :] = pair[:, 0, :].astype(own.dtype)
        own[1, rows, :] = pair[:, 1, :].astype(own.dtype)

    pl.semaphore_wait(barrier, n * n - 1)

    def up(s):
        return remote(mine_part(0, s), part_of(chain, c, s), up_send.at[0, s], chain_recv.at[c, s], r, c + 1)

    def down(s):
        return remote(mine_part(1, s), part_of(chain, c, s), up_send.at[1, s], chain_recv.at[c, s], r, c - 1)

    ahead = 2
    for s in chunks:
        first = s < ahead
        pl.when(c < n - 1 if first else c == 0)(lambda: up(s).start())
        pl.when(c > 0 if first else c == n - 1)(lambda: down(s).start())

    def right_copy(k):
        h = jnp.where(k < c, 0, 1)
        return remote(mine_at(h), right.at[r], right_send.at[k], right_recv.at[r], k, c)

    def left_copy(k, s):
        return remote(
            part_of(chain, k, s), part_of(left, r, s), left_send.at[k, s], left_recv.at[r, s], k, c
        )

    def own_left_copy(s):
        return remote(
            mine_part(0, s), part_of(left, r, s), left_send.at[c, s], left_recv.at[r, s], c, c
        )

    for step in range(1, n):
        right_copy(lax.rem(r + step, n)).start()
    for s in chunks:
        pl.when(off)(lambda: own_left_copy(s).start())

    def gq_copy(j):
        return remote(gains, gq0.at[c], gq_send.at[j], gq_recv.at[c], r, j)

    def gp_copy(i):
        return remote(gains, gp0.at[c], gp_send.at[i], gp_recv.at[c], i, r)

    for k in range(n):
        pl.when(k != c)(lambda k=k: gq_copy(k).start())
        pl.when(jnp.logical_or(k != r, off))(lambda k=k: gp_copy(k).start())
    gq0[c] = gains[...]

    @pl.when(diag)
    def _():
        gp0[c] = gains[...]

    sky_copy.wait()

    rows_step = 32
    lane = lax.broadcasted_iota(jnp.int32, (rows_step, block), 1) + c * block
    sub = lax.broadcasted_iota(jnp.int32, (rows_step, block), 0) + r * block

    @pl.loop(0, block // rows_step)
    def _(s):
        rows = pl.ds(pl.multiple_of(s * rows_step, rows_step), rows_step)
        pair = sky[rows].astype(jnp.float32)
        mr, mi = pair[:, 0, :], pair[:, 1, :]
        keep = sub + s * rows_step != lane
        mr = jnp.where(keep, mr, 0.0)
        mi = jnp.where(keep, mi, 0.0)
        model[0, rows, :] = mr
        model[1, rows, :] = mi
        power[rows, :] = mr * mr + mi * mi
        vr[rows, :] = jnp.zeros((rows_step, block), jnp.float32)
        vi[rows, :] = jnp.zeros((rows_step, block), jnp.float32)

    mine = pltpu.make_async_copy(mine_at(jnp.where(r < c, 0, 1)), right.at[r], local_sem.at[1])
    mine.start()
    mine.wait()

    def multiply(a_ref, b_ref, k, s):
        rows = pl.ds(pl.multiple_of(s * tile, tile), tile)
        ar, ai = a_ref[k, 0, rows, :], a_ref[k, 1, rows, :]
        br, bi = b_ref[k, 0], b_ref[k, 1]
        dot = functools.partial(
            lax.dot_general, dimension_numbers=CONTRACT_LAST, preferred_element_type=jnp.float32
        )
        both = lambda x, y: jnp.concatenate([x, y], axis=1)
        found = dot(jnp.concatenate([both(ar, ai), both(ai, -ar)], axis=0), both(br, bi))
        vr[rows, :] += found[:tile]
        vi[rows, :] += found[tile:]

    def square(ref, k):
        @pl.loop(0, len(chunks))
        def _(s):
            multiply(ref, ref, k, s)

    @pl.when(diag)
    def _():
        copy = pltpu.make_async_copy(mine_at(0), left.at[r], local_sem.at[0])
        copy.start()
        copy.wait()

        square(left, r)
        square(right, r)

    def onward_copy(k, s, onward):
        return remote(
            part_of(chain, k, s), part_of(chain, k, s), fwd_send.at[k, s], chain_recv.at[k, s], r, c + onward
        )

    def arrived(k, s, onward):
        landed(part_of(chain, k, s), chain_recv.at[k, s])
        pl.when(jnp.logical_and(c + onward >= 0, c + onward < n))(lambda: onward_copy(k, s, onward).start())
        pl.when(k != r)(lambda: left_copy(k, s).start())

    for s in chunks:
        for step in range(1, n):
            pl.when(c >= step)(lambda: arrived(c - step, s, 1))
            pl.when(c + step < n)(lambda: arrived(c + step, s, -1))
            if step == 1 and s + ahead < len(chunks):
                inner = jnp.logical_and(c > 0, c < n - 1)
                pl.when(inner)(lambda: up(s + ahead).start())
                pl.when(inner)(lambda: down(s + ahead).start())

    @pl.when(off)
    def _():
        @pl.loop(0, len(chunks))
        def _(s):
            multiply(chain, right, r, s)

    for k in range(n):
        pl.when(k != c)(lambda k=k: landed(gq0.at[k], gq_recv.at[k]))
        pl.when(jnp.logical_or(k != c, off))(lambda k=k: landed(gp0.at[k], gp_recv.at[k]))

    def start_gains(ref):
        return [jnp.concatenate([ref[k, part : part + 1, :] for k in range(n)], axis=1) for part in range(2)]

    gp = start_gains(gp0)
    gq = start_gains(gq0)
    lanes = 128

    def lay_out(gains_row):
        qr[...] = jnp.broadcast_to(gains_row[0], (lanes, block)).T
        qi[...] = jnp.broadcast_to(gains_row[1], (lanes, block)).T

    lay_out(gq)

    @pl.when(off)
    def _():
        for step in range(1, n):
            k = lax.rem(r + step, n)
            landed(right.at[k], right_recv.at[k])

        @pl.loop(0, len(chunks))
        def _(s):
            @pl.loop(1, n)
            def _(step):
                k = lax.rem(r + step, n)
                rows = pl.ds(pl.multiple_of(s * tile, tile), tile)
                landed(left.at[k, :, rows, :], left_recv.at[k, s])
                multiply(left, right, k, s)

    @pl.when(diag)
    def _():
        @pl.loop(1, n)
        def _(step):
            k = lax.rem(r + step, n)
            landed(right.at[k], right_recv.at[k])
            square(right, k)

        @pl.loop(1, n)
        def _(step):
            k = lax.rem(r + step, n)
            for s in chunks:
                landed(part_of(left, k, s), left_recv.at[k, s])
            square(left, k)

    @pl.loop(0, block // rows_step)
    def _(s):
        rows = pl.ds(pl.multiple_of(s * rows_step, rows_step), rows_step)
        mr, mi = model[0, rows, :], model[1, rows, :]
        a, b = vr[rows, :], vi[rows, :]
        vr[rows, :] = a * mr + b * mi
        vi[rows, :] = a * mi - b * mr

    for it in range(ITERS):
        if it > 0:
            lay_out(gq)
        width = max(block // 2, lanes)
        for start in range(0, block, width):
            columns = pl.ds(start, width)
            gpr = jnp.broadcast_to(gp[0][:, start : start + width], (8, width))
            gpi = jnp.broadcast_to(gp[1][:, start : start + width], (8, width))

            def fold(x):
                total = x[:, :lanes]
                for t in range(lanes, width, lanes):
                    total = total + x[:, t : t + lanes]
                return total

            def sums(s, carry):
                sum_r, sum_i, sum_e = carry
                rows = pl.ds(pl.multiple_of(s * 8, 8), 8)
                wr, wi = vr[rows, columns], vi[rows, columns]
                ar, ai = qr[rows, :], qi[rows, :]
                norm = ar * ar + ai * ai
                wide = lambda x: jnp.concatenate([x] * (width // lanes), axis=1)
                ar, ai, norm = wide(ar), wide(ai), wide(norm)
                row_r = fold(wr * gpr + wi * gpi)
                row_i = fold(wr * gpi - wi * gpr)
                if start > 0:
                    row_r = row_r + tr[rows, :]
                    row_i = row_i + ti[rows, :]
                tr[rows, :] = row_r
                ti[rows, :] = row_i
                return (
                    sum_r + (wr * ar - wi * ai),
                    sum_i + (wr * ai + wi * ar),
                    sum_e + power[rows, columns] * norm,
                )

            zero = jnp.zeros((8, width), jnp.float32)
            found = lax.fori_loop(0, block // 8, sums, (zero, zero, zero), unroll=4)
            for part, value in enumerate(found):
                abuf[it, part : part + 1, columns] = jnp.sum(value, axis=0, keepdims=True)
        for part, ref in enumerate((tr, ti)):
            bbuf[it, part : part + 1, :] = jnp.sum(ref[...].T, axis=0, keepdims=True)

        a_copy = remote(abuf.at[it], ain.at[it, r], a_send.at[it], a_recv.at[it, r], c, c)
        b_copy = remote(bbuf.at[it], bin_.at[it, c], b_send.at[it], b_recv.at[it, c], r, r)

        @pl.when(off)
        def _():
            a_copy.start()
            b_copy.start()

        def p_copy(i):
            return remote(gin.at[it, 0], gin.at[it, 0], g_send.at[it, 0, i], g_recv.at[it, 0], i, c)

        def q_copy(j):
            return remote(gin.at[it, 0], gin.at[it, 1], g_send.at[it, 1, j], g_recv.at[it, 1], r, j)

        @pl.when(diag)
        def _():
            total = abuf[it]
            for k in range(n):
                @pl.when(k != r)
                def _():
                    landed(ain.at[it, k], a_recv.at[it, k])
                    landed(bin_.at[it, k], b_recv.at[it, k])

            ain[it, r] = jnp.zeros_like(total)
            bin_[it, r] = jnp.zeros((2, block), jnp.float32)
            for k in range(n):
                total = total + ain[it, k]
            extra = bin_[it, 0]
            for k in range(1, n):
                extra = extra + bin_[it, k]
            for part in range(2):
                fresh = (total[part : part + 1] + extra[part : part + 1]) / total[2:3]
                if it == 1:
                    fresh = 0.5 * (fresh + gin[0, 0, part : part + 1, :])
                gin[it, 0, part : part + 1, :] = fresh
                gin[it, 1, part : part + 1, :] = fresh
            for k in range(n):
                @pl.when(k != r)
                def _():
                    q_copy(k).start()
                    if it < ITERS - 1:
                        p_copy(k).start()

        @pl.when(off)
        def _():
            landed(gin.at[it, 1], g_recv.at[it, 1])
            if it < ITERS - 1:
                landed(gin.at[it, 0], g_recv.at[it, 0])

        gp = [gin[it, 0, part : part + 1, :] for part in range(2)]
        gq = [gin[it, 1, part : part + 1, :] for part in range(2)]

    out[...] = gin[ITERS - 1, 1, 0:2, pl.ds(pl.multiple_of(c * share, share), share)]

    for step in range(1, n):
        right_copy(lax.rem(r + step, n)).wait_send()

    def gone(k, s, onward):
        pl.when(jnp.logical_and(c + onward >= 0, c + onward < n))(lambda: onward_copy(k, s, onward).wait_send())
        pl.when(k != r)(lambda: left_copy(k, s).wait_send())

    for s in chunks:
        pl.when(c < n - 1)(lambda: up(s).wait_send())
        pl.when(c > 0)(lambda: down(s).wait_send())
        pl.when(off)(lambda: own_left_copy(s).wait_send())
        for step in range(1, n):
            pl.when(c >= step)(lambda: gone(c - step, s, 1))
            pl.when(c + step < n)(lambda: gone(c + step, s, -1))
    for k in range(n):
        pl.when(k != c)(lambda k=k: gq_copy(k).wait_send())
        pl.when(jnp.logical_or(k != r, off))(lambda k=k: gp_copy(k).wait_send())
    for it in range(ITERS):
        a_copy = remote(abuf.at[it], ain.at[it, r], a_send.at[it], a_recv.at[it, r], c, c)
        b_copy = remote(bbuf.at[it], bin_.at[it, c], b_send.at[it], b_recv.at[it, c], r, r)

        @pl.when(off)
        def _():
            a_copy.wait_send()
            b_copy.wait_send()

        for k in range(n):
            @pl.when(jnp.logical_and(diag, k != r))
            def _():
                remote(gin.at[it, 0], gin.at[it, 1], g_send.at[it, 1, k], g_recv.at[it, 1], r, k).wait_send()
                if it < ITERS - 1:
                    remote(gin.at[it, 0], gin.at[it, 0], g_send.at[it, 0, k], g_recv.at[it, 0], k, c).wait_send()


def square_body(n, samples, sky_model, initial_gains):
    block, _, times = samples.shape
    half = times // 2
    share = initial_gains.shape[1]
    dma = pltpu.SemaphoreType.DMA
    vmem = pltpu.VMEM
    f32, bf16 = jnp.float32, jnp.bfloat16
    piece = (n, 2, block, half)
    return pl.pallas_call(
        functools.partial(calibrate, n),
        out_shape=jax.ShapeDtypeStruct((2, share), f32),
        in_specs=[
            pl.BlockSpec(memory_space=pltpu.VMEM),
            pl.BlockSpec(memory_space=pl.ANY),
            pl.BlockSpec(memory_space=pltpu.VMEM),
        ],
        out_specs=pl.BlockSpec(memory_space=pltpu.VMEM),
        scratch_shapes=[
            vmem((2, block, times), bf16),
            vmem(sky_model.shape, bf16),
            vmem(piece, bf16),
            vmem(piece, bf16),
            vmem(piece, bf16),
            vmem((block, block), f32),
            vmem((block, block), f32),
            vmem((block, block), f32),
            vmem((2, block, block), f32),
            vmem((block, 128), f32),
            vmem((block, 128), f32),
            vmem((block, 128), f32),
            vmem((block, 128), f32),
            vmem((n, 2, share), f32),
            vmem((n, 2, share), f32),
            vmem((ITERS, 4, block), f32),
            vmem((ITERS, 2, block), f32),
            vmem((ITERS, n, 4, block), f32),
            vmem((ITERS, n, 2, block), f32),
            vmem((ITERS, 2, 2, block), f32),
            dma((2, CHUNKS)), dma((n, CHUNKS)), dma((n, CHUNKS)),
            dma((n, CHUNKS)), dma((n, CHUNKS)), dma((n,)), dma((n,)), dma((2,)),
            dma((n,)), dma((n,)), dma((n,)), dma((n,)),
            dma((ITERS,)), dma((ITERS, n)), dma((ITERS,)), dma((ITERS, n)),
            dma((ITERS, 2, n)), dma((ITERS, 2)),
        ],
        compiler_params=pltpu.CompilerParams(
            collective_id=0, has_side_effects=True, vmem_limit_bytes=56 * 1024 * 1024
        ),
        cost_estimate=pl.CostEstimate(
            flops=8 * block * block * times * n // 2, bytes_accessed=8 * block * block, transcendentals=0
        ),
    )(samples, sky_model, initial_gains)


def body(samples, sky_model, initial_gains):
    row_count = lax.axis_size("row")
    column_count = lax.axis_size("col")
    row_index = lax.axis_index("row")
    column_index = lax.axis_index("col")
    block_column = samples.shape[0]
    block_row = sky_model.shape[0]
    share_size = initial_gains.shape[1]
    contract_last = (((1,), (1,)), ((), ()))
    upper_limit = lax.Precision.HIGHEST
    own_start = (row_index * column_count + column_index) * share_size
    flattened = samples.reshape(block_column, -1)
    rotated = jnp.concatenate([-samples[:, 1, :], samples[:, 0, :]], axis=1)
    right_side = jnp.concatenate([flattened, rotated], axis=0)
    all_antennas = lax.all_gather(flattened, "col", axis=0, tiled=True)
    vis_tile = lax.psum_scatter(
        lax.dot_general(
            all_antennas, right_side, contract_last, preferred_element_type=jnp.float32
        ),
        "row",
        scatter_dimension=0,
        tiled=True,
    )
    vis_real = vis_tile[:, :block_column]
    vis_imag = vis_tile[:, block_column:]
    model_real = sky_model[:, 0, :].astype(jnp.float32)
    model_imag = sky_model[:, 1, :].astype(jnp.float32)
    global_rows = row_index * block_row + lax.broadcasted_iota(
        jnp.int32, (block_row, block_column), 0
    )
    global_columns = column_index * block_column + lax.broadcasted_iota(
        jnp.int32, (block_row, block_column), 1
    )
    cross_mask = (global_rows != global_columns).astype(jnp.float32)
    weight_real = (vis_real * model_real + vis_imag * model_imag) * cross_mask
    weight_imag = (vis_real * model_imag - vis_imag * model_real) * cross_mask
    model_power = (model_real * model_real + model_imag * model_imag) * cross_mask
    stacked = jnp.concatenate([weight_real, weight_imag], axis=0)
    row_gains = lax.all_gather(initial_gains, "col", axis=1, tiled=True)
    everything = row_gains
    for iteration in range(ITERS):
        gain_real = row_gains[0]
        gain_imag = row_gains[1]
        left_rows = jnp.stack(
            [jnp.concatenate([gain_real, -gain_imag]), jnp.concatenate([gain_imag, gain_real])]
        )
        totals = jnp.dot(left_rows, stacked, precision=upper_limit)
        energy = jnp.dot(
            gain_real * gain_real + gain_imag * gain_imag, model_power, precision=upper_limit
        )
        totals, energy = (totals, energy)
        totals, energy = (
            lax.psum_scatter(totals, "row", scatter_dimension=1, tiled=True),
            lax.psum_scatter(energy, "row", scatter_dimension=0, tiled=True),
        )
        updated = totals / energy[None, :]
        if iteration == 1:
            previous = lax.dynamic_slice_in_dim(
                everything, (column_index * row_count + row_index) * share_size, share_size, 1
            )
            updated = 0.5 * (updated + previous)
        gain_block = lax.all_gather(updated, "row", axis=1, tiled=True)
        everything = lax.all_gather(gain_block, "col", axis=1, tiled=True)
        row_gains = lax.dynamic_slice_in_dim(everything, row_index * block_row, block_row, 1)
    return lax.dynamic_slice_in_dim(everything, own_start, share_size, 1)


def solution(mesh):
    n = mesh.shape["row"]
    square = n == mesh.shape["col"]
    return jax.shard_map(
        functools.partial(square_body, n) if square else body,
        mesh=mesh,
        in_specs=(
            P(("chan", "col"), None, "row"),
            P(("chan", "row"), None, "col"),
            P(None, ("chan", "row", "col")),
        ),
        out_specs=P(None, ("chan", "row", "col")),
        check_vma=False,
    )
```
